256 devices in a mesh: space: 64 (over z, x_hi, y), freq: 4 (over x_lo, core).
Axes of the slice: x: 4 (x_hi: 2, x_lo: 2; x = x_hi * 2 + x_lo), y: 4, z: 8, core: 2. Of those that a mesh axis runs over, the one named last changes fastest.
Arguments:
- forcing: bfloat16 [4, 32, 8, 64, 1536], P(None, 'freq', None, 'space'), may hold values from -36 to 36
- base_harm: float32 [7, 2, 64, 1536], P(None, None, 'space'), may hold values from -6 to 6
- mixing: float32 [7, 4, 4], replicated, may hold values from -3 to 3
- mean_flow: float32 [1536], replicated, may hold values from 0.2 to 1.2
- harm_lo: int32 [1], replicated, may hold values from -20 to -9
- couple_flags: int32 [32, 7], P('freq'), may hold values 0 or 1
Outputs:
- response: bfloat16 [4, 32, 8, 64, 1536], P(None, 'freq', None, 'space')
- gram_matrix: float32 [4, 4], replicated
The draws below stay inside these ranges and needn't reach their ends.
All inputs are finite; a program needn't handle non-finite values. No bound on the sum of `couple_flags` on one device may be relied on, other than what follows from the above.
Results may differ from the reference program's by a relative error of at most 0.004.
Values may be sent and summed in bfloat16 or wider, within the bound.
A program may use at most 128 MiB of HBM per device.

```python
import jax
import jax.numpy as jnp
from jax import lax

S = 4
H = 32
V = 4
MODES = 7
NY = 32
NZ = 48
NX = 64
NYZ = 1536


def draw_forcing(key, part):
    first = jax.random.fold_in(key, 0)
    dims_all = (S, H, 2 * V, NX, NY * NZ)
    rise_x = 1.0 + 2.0 * jnp.arange(NX, dtype=jnp.float32) / (NX - 1)
    rise_h = 1.0 + 2.0 * jnp.arange(H, dtype=jnp.float32) / (H - 1)
    scaling = rise_h[None, :, None, None, None] * rise_x[None, None, None, :, None]
    values = jnp.clip(jax.random.normal(first, dims_all, jnp.float32), -4.0, 4.0) * scaling
    return values.astype(jnp.bfloat16)


def plant(entries, own_key, low, largest):
    index_at = [jax.random.randint(jax.random.fold_in(own_key, axis), (), 0, length) for axis, length in enumerate(entries.shape)]
    longest = entries.shape.index(max(entries.shape))
    neighbour = index_at[:longest] + [(index_at[longest] + 1) % entries.shape[longest]] + index_at[longest + 1:]
    return entries.at[tuple(index_at)].set(low).at[tuple(neighbour)].set(largest)


def block_levels(key, shape, pieces, low, high):
    gain = 1.0
    for dim, blocks in pieces:
        draws = jax.random.uniform(jax.random.fold_in(jax.random.fold_in(key, 6), dim), (blocks,), jnp.float32, low / len(pieces), high / len(pieces))
        gain = gain * jnp.repeat(jnp.exp(draws), shape[dim] // blocks).reshape((-1,) + (1,) * (len(shape) - 1 - dim))
    return gain


def centred(stream_key, dims, scale, reach, shards=(), kind=jnp.bfloat16):
    entries = scale * jax.random.normal(stream_key, dims, jnp.float32)
    if shards:
        entries = entries * block_levels(stream_key, dims, shards, -0.22, 0.18)
    return jnp.clip(entries, -reach, reach).astype(kind)


def setup_inputs(seed: int = 0) -> dict:
    key_list = jax.random.split(jax.random.key(seed), 7)
    forcing = draw_forcing(jax.random.fold_in(key_list[6], 71), 0)
    base_harm = centred(key_list[1], (MODES, 2, NX, NYZ), 0.4, 6.0, ((2, 64),), jnp.float32)
    mixing = centred(key_list[2], (MODES, V, V), V ** -0.5, 3.0, (), jnp.float32)
    mean_flow = jnp.clip(jax.random.uniform(key_list[3], (NYZ,), jnp.float32, 0.2, 1.2), 0.2, 1.2)
    harm_lo = jax.random.randint(key_list[4], (1,), -20, -8).astype(jnp.int32)
    couple_flags = plant((jax.random.randint(key_list[5], (H, MODES), 0, 4) < 3).astype(jnp.int32), jax.random.fold_in(key_list[5], 1), 0, 1)
    return dict(forcing=forcing, base_harm=base_harm, mixing=mixing, mean_flow=mean_flow, harm_lo=harm_lo, couple_flags=couple_flags)


OMEGA = 0.05
VISCOSITY = 0.25


def crossflow(values, stream):
    cells = NY * NZ
    position = jnp.arange(cells, dtype=jnp.int32)
    span_pos = position % NZ
    wake_pos = position // NZ
    span_up = jnp.where(span_pos == NZ - 1, jnp.roll(values, NZ - 1, -1), jnp.roll(values, -1, -1))
    span_down = jnp.where(span_pos == 0, jnp.roll(values, 1 - NZ, -1), jnp.roll(values, 1, -1))
    wake_up = jnp.where(wake_pos == NY - 1, 0.0, jnp.roll(values, -NZ, -1))
    wake_down = jnp.where(wake_pos == 0, 0.0, jnp.roll(values, NZ, -1))
    return VISCOSITY * (wake_up + wake_down + span_up + span_down - 6.0 * values)


def streamwise(left_vals, right_vals, stream):
    return (VISCOSITY + 0.5 * stream) * left_vals + (VISCOSITY - 0.5 * stream) * right_vals


def rotation(values, frequency):
    spin_rate = (OMEGA * frequency)[:, None, None, None]
    real_part = values[..., :V, :, :]
    imag_part = values[..., V:, :, :]
    return jnp.concatenate([-spin_rate * imag_part, spin_rate * real_part], axis=-3)


def coupling(padded, base_modes, mixing, couplers):
    count_h = couplers.shape[0]
    summed = None
    for j in range(7):
        offset = j - 3
        source = lax.slice_in_dim(padded, 3 - offset, 3 - offset + count_h, axis=padded.ndim - 4)
        halves = source.reshape(source.shape[:-3] + (2, V) + source.shape[-2:])
        blended = jnp.einsum("vw,...cwxn->...cvxn", mixing[j], halves, precision=lax.Precision.HIGHEST)
        base_re = base_modes[j, 0]
        base_im = base_modes[j, 1]
        mix_re = blended[..., 0, :, :, :]
        mix_im = blended[..., 1, :, :, :]
        product_term = jnp.stack([base_re * mix_re - base_im * mix_im, base_re * mix_im + base_im * mix_re], axis=-4)
        weights = couplers[:, j].astype(jnp.float32)[:, None, None, None, None]
        contrib = weights * product_term
        summed = contrib if summed is None else summed + contrib
    return summed.reshape(summed.shape[:-5] + (count_h, 2 * V) + summed.shape[-2:])


def one_forcing(values, base_modes, mixing, couplers, stream, frequency):
    widened = values.astype(jnp.float32)
    zero_plane = jnp.zeros_like(widened[:, :, :1])
    left_vals = jnp.concatenate([zero_plane, widened[:, :, :-1]], axis=2)
    right_vals = jnp.concatenate([widened[:, :, 1:], zero_plane], axis=2)
    spatial = crossflow(widened, stream) + streamwise(left_vals, right_vals, stream)
    padded = jnp.pad(widened, ((3, 3), (0, 0), (0, 0), (0, 0)))
    result = rotation(widened, frequency) - spatial - coupling(padded, base_modes, mixing, couplers)
    return result.astype(jnp.bfloat16)


def reference(forcing, base_harm, mixing, mean_flow, harm_lo, couple_flags):
    frequency = (harm_lo[0] + jnp.arange(H, dtype=jnp.int32)).astype(jnp.float32)
    response = lax.map(lambda item: one_forcing(item, base_harm, mixing, couple_flags, mean_flow, frequency), forcing)
    flattened = response.reshape(S, -1)
    cells_all = H * 2 * V * NX * NY * NZ
    gram_matrix = jnp.dot(flattened, flattened.T, preferred_element_type=jnp.float32) / cells_all
    return response, gram_matrix
```

```python
import functools

import jax
import jax.numpy as jnp
from jax import lax
from jax.experimental import pallas as pl
from jax.experimental.pallas import tpu as pltpu
from jax.sharding import PartitionSpec as P

MESH = pl.DeviceIdType.MESH
S, K, C, N = 4, 8, 8, 1536
ROWS = K * C
NZ = 48
OMEGA = 0.05
VISCOSITY = 0.25
CHUNKS = 4
CROWS = ROWS // CHUNKS
RIM = 3 * C
LANES = 256

OWN = [(j, k, k - j + 3) for k in range(K) for j in range(7) if 0 <= k - j + 3 < K]
LEFT = [(j, k, k - j + 6) for k in range(3) for j in range(7) if k - j + 3 < 0]
RIGHT = [(j, k, k - j + 3 - K) for k in range(K - 3, K) for j in range(7) if k - j + 3 >= K]

PAIRS = [(s, t) for s in range(S) for t in range(s, S)]


def split(coeff):
    high = coeff.astype(jnp.bfloat16)
    low = (coeff - high.astype(jnp.float32)).astype(jnp.bfloat16)
    return high, low


def swapped(value):
    return jnp.concatenate([value[4:], value[:4]], axis=0)


def pair_iota(width):
    row = lax.broadcasted_iota(jnp.int32, (C, width), 0)
    col = lax.broadcasted_iota(jnp.int32, (C, width), 1)
    return row, col


def mixing_tile(mix_ref, j, width):
    row, col = pair_iota(width)
    same = (row // 4) == ((col // 4) % 2)
    tile = jnp.zeros((C, width), jnp.float32)
    for v in range(4):
        for w in range(4):
            hit = same & (row % 4 == v) & (col % 4 == w)
            tile = jnp.where(hit, mix_ref[v, w, j], tile)
    return tile


def halo_kernel(
    f_ref, blocks_ref, base_ref, mean_ref, mix_hbm, lo_hbm, flag_hbm, resp_ref, part_ref,
    mix_ref, lo_ref, flag_ref,
    x_ref, from_left, from_right, rim_in, base_in, mean_in, re_ref, im_ref,
    acc_ref, out_ref, own_coeff, rim_coeff, mixed_ref, rim_mixed, gram_ref,
    in_sem, out_sem, send_sem, recv_sem, rim_send, rim_recv,
):
    sp, fr = lax.axis_index("space"), lax.axis_index("freq")
    has_l, has_r = sp > 0, sp < lax.axis_size("space") - 1
    has_d, has_u = fr > 0, fr < lax.axis_size("freq") - 1
    to_l, to_r = {"space": sp - 1}, {"space": sp + 1}
    to_d, to_u = {"freq": fr - 1}, {"freq": fr + 1}
    greeted = ((has_l, to_l), (has_r, to_r), (has_d, to_d), (has_u, to_u))

    barrier = pltpu.get_barrier_semaphore()
    for there, device in greeted:

        @pl.when(there)
        def _():
            pl.semaphore_signal(barrier, inc=1, device_id=device, device_id_type=MESH)

    load_x = pltpu.make_async_copy(f_ref, x_ref, in_sem.at[0])
    load_base = pltpu.make_async_copy(base_ref, base_in, in_sem.at[1])
    load_mean = pltpu.make_async_copy(mean_ref, mean_in, in_sem.at[2])
    loads = [load_x, load_base, load_mean]
    for i, (source, target) in enumerate(
        ((mix_hbm, mix_ref), (lo_hbm, lo_ref), (flag_hbm, flag_ref))
    ):
        loads.append(pltpu.make_async_copy(source, target, in_sem.at[3 + i]))
    for load in loads:
        load.start()
    peers = sum(there.astype(jnp.int32) for there, _ in greeted)
    pl.semaphore_wait(barrier, peers)

    def plane_copy(way, part):
        rows = pl.ds(part * CROWS, CROWS)
        landing = from_left if way == 0 else from_right
        return pltpu.make_async_remote_copy(
            src_ref=f_ref.at[:, rows],
            dst_ref=landing.at[:, rows],
            send_sem=send_sem.at[way, part],
            recv_sem=recv_sem.at[way, part],
            device_id=to_r if way == 0 else to_l,
            device_id_type=MESH,
        )

    def rim_copy(way):
        return pltpu.make_async_remote_copy(
            src_ref=blocks_ref.at[:, K - 3 : K] if way == 0 else blocks_ref.at[:, 0:3],
            dst_ref=rim_in.at[way],
            send_sem=rim_send.at[way],
            recv_sem=rim_recv.at[way],
            device_id=to_u if way == 0 else to_d,
            device_id_type=MESH,
        )

    for way, there in ((0, has_u), (1, has_d)):

        @pl.when(there)
        def _():
            rim_copy(way).start()

    for part in range(CHUNKS):
        for way, there in ((0, has_r), (1, has_l)):

            @pl.when(there)
            def _():
                plane_copy(way, part).start()

    for way, there in ((0, has_d), (1, has_u)):

        @pl.when(jnp.logical_not(there))
        def _():
            rim_in[way] = jnp.zeros((S, 3, C, N), jnp.bfloat16)

    for landing, there in ((from_left, has_l), (from_right, has_r)):

        @pl.when(jnp.logical_not(there))
        def _():
            landing[...] = jnp.zeros((S, ROWS, N), jnp.bfloat16)

    for load in loads:
        load.wait()
    width = S * RIM
    row, col = pair_iota(width)
    for j in range(7):
        tile = mixing_tile(mix_ref, j, width)
        for slot, (jj, k, source) in enumerate(OWN):
            if jj == j:
                flag = flag_ref[k, j].astype(jnp.float32)
                block = jnp.where(col // C == source, tile, 0.0) * flag
                own_coeff[slot * C : slot * C + C, :] = block[:, :ROWS]
        for way, listed in ((0, LEFT), (1, RIGHT)):
            for slot, (jj, k, source) in enumerate(listed):
                if jj == j:
                    flag = flag_ref[k, j].astype(jnp.float32)
                    for s in range(S):
                        at = (s * len(listed) + slot) * C
                        block = jnp.where(col // C == 3 * s + source, tile, 0.0) * flag
                        rim_coeff[way, at : at + C, :] = block

    for j in range(7):
        re_ref[j] = jnp.broadcast_to(base_in[j, 0], (C, N))
        im_ref[j] = jnp.broadcast_to(base_in[j, 1], (C, N))

    own_high, own_low = split(own_coeff[...])
    own_both = jnp.concatenate([own_high, own_low], axis=1)
    sign = jnp.where(lax.broadcasted_iota(jnp.int32, (C, N), 0) < 4, 1.0, -1.0).astype(jnp.float32)
    first = lo_ref[0] + fr * K

    place = lax.broadcasted_iota(jnp.int32, (C, N), 1)
    span = place % NZ
    span_last, span_first = span == NZ - 1, span == 0
    wake_last, wake_first = place >= N - NZ, place < NZ

    def local_part(s, carry):
        values = x_ref[s]
        mixed_ref[...] = jnp.dot(
            own_both,
            jnp.concatenate([values, values], axis=0),
            preferred_element_type=jnp.float32,
        )
        for k in range(K):
            if k % 2 == 0:
                both = x_ref[s, k * C : k * C + 2 * C].astype(jnp.float32)
            x = both[(k % 2) * C : (k % 2) * C + C]
            up, down = pltpu.roll(x, N - 1, 1), pltpu.roll(x, 1, 1)
            span_up = jnp.where(span_last, pltpu.roll(x, NZ - 1, 1), up)
            span_down = jnp.where(span_first, pltpu.roll(x, N - NZ + 1, 1), down)
            wake_up = jnp.where(wake_last, 0.0, pltpu.roll(x, N - NZ, 1))
            wake_down = jnp.where(wake_first, 0.0, pltpu.roll(x, NZ, 1))
            around = VISCOSITY * (wake_up + wake_down + span_up + span_down - 6.0 * x)
            spin = OMEGA * (first + k).astype(jnp.float32)
            turned = spin * x
            straight = around
            for slot, (j, kk, _source) in enumerate(OWN):
                if kk == k:
                    mixed = mixed_ref[slot * C : slot * C + C, :]
                    straight = straight + re_ref[j] * mixed
                    turned = turned - im_ref[j] * mixed
            acc_ref[s, k * C : k * C + C] = swapped(sign * turned) - straight
        return carry

    lax.fori_loop(0, S, local_part, 0)

    for way, there, listed in ((0, has_d, LEFT), (1, has_u, RIGHT)):

        @pl.when(there)
        def _():
            rim_copy(way).wait_recv()

        high, low = split(rim_coeff[way])
        rim = rim_in[way].astype(jnp.float32).reshape(S * RIM, N).astype(jnp.bfloat16)
        rim_mixed[...] = jnp.dot(high, rim, preferred_element_type=jnp.float32) + jnp.dot(
            low, rim, preferred_element_type=jnp.float32
        )

        def rim_part(s, carry):
            for k in sorted({k for _, k, _ in listed}):
                straight = turned = None
                for slot, (j, kk, _source) in enumerate(listed):
                    if kk == k:
                        at = pl.multiple_of((s * len(listed) + slot) * C, C)
                        mixed = rim_mixed[pl.ds(at, C), :]
                        a, b = re_ref[j] * mixed, im_ref[j] * mixed
                        straight = a if straight is None else straight + a
                        turned = b if turned is None else turned + b
                acc_ref[s, k * C : k * C + C] -= swapped(sign * turned) + straight
            return carry

        lax.fori_loop(0, S, rim_part, 0)

    gram_ref[...] = jnp.zeros_like(gram_ref)
    half = 0.5 * mean_in[...].reshape(1, N)
    for part in range(CHUNKS):
        rows = slice(part * CROWS, (part + 1) * CROWS)
        for way, there in ((0, has_l), (1, has_r)):

            @pl.when(there)
            def _():
                plane_copy(way, part).wait_recv()

        sums = [gram_ref[p] for p in range(len(PAIRS))]
        for at in range(0, N, LANES):
            lanes = slice(at, at + LANES)
            gain_l = VISCOSITY + half[:, lanes]
            gain_r = VISCOSITY - half[:, lanes]
            rounded = []
            for s in range(S):
                left = from_left[s, rows, lanes].astype(jnp.float32)
                right = from_right[s, rows, lanes].astype(jnp.float32)
                value = acc_ref[s, rows, lanes] - (gain_l * left + gain_r * right)
                value = value.astype(jnp.bfloat16)
                out_ref[s, rows, lanes] = value
                rounded.append(value.astype(jnp.float32))
            for p, (s, t) in enumerate(PAIRS):
                product = rounded[s] * rounded[t]
                sums[p] = sums[p] + (product[:C] + product[C:])
        for p in range(len(PAIRS)):
            gram_ref[p] = sums[p]
        pltpu.make_async_copy(
            out_ref.at[:, rows], resp_ref.at[:, rows], out_sem.at[part]
        ).start()

    row, col = pair_iota(128)
    tile = jnp.zeros((C, 128), jnp.float32)
    for p, (s, t) in enumerate(PAIRS):
        total = jnp.sum(gram_ref[p])
        hit = ((row == s) & (col == t)) | ((row == t) & (col == s))
        tile = jnp.where(hit, total, tile)
    part_ref[...] = tile

    for part in range(CHUNKS):
        rows = slice(part * CROWS, (part + 1) * CROWS)
        pltpu.make_async_copy(
            out_ref.at[:, rows], resp_ref.at[:, rows], out_sem.at[part]
        ).wait()
        for way, there in ((0, has_r), (1, has_l)):

            @pl.when(there)
            def _():
                plane_copy(way, part).wait_send()

    for way, there in ((0, has_u), (1, has_d)):

        @pl.when(there)
        def _():
            rim_copy(way).wait_send()


def apply_operator(forcing, base_harm, mean_flow, mixing, harm_lo, couple_flags):
    any_ = pl.BlockSpec(memory_space=pl.ANY)
    bf16, f32 = jnp.bfloat16, jnp.float32
    return pl.pallas_call(
        halo_kernel,
        out_shape=(
            jax.ShapeDtypeStruct((S, ROWS, N), bf16),
            jax.ShapeDtypeStruct((C, 128), f32),
        ),
        in_specs=[any_] * 7,
        out_specs=(any_, pl.BlockSpec(memory_space=pltpu.VMEM)),
        scratch_shapes=[
            pltpu.SMEM((4, 4, 7), f32),
            pltpu.SMEM((1,), jnp.int32),
            pltpu.SMEM((K, 7), jnp.int32),
            pltpu.VMEM((S, ROWS, N), bf16),
            pltpu.VMEM((S, ROWS, N), bf16),
            pltpu.VMEM((S, ROWS, N), bf16),
            pltpu.VMEM((2, S, 3, C, N), bf16),
            pltpu.VMEM((7, 2, 1, N), f32),
            pltpu.VMEM((N,), f32),
            pltpu.VMEM((7, C, N), f32),
            pltpu.VMEM((7, C, N), f32),
            pltpu.VMEM((S, ROWS, N), f32),
            pltpu.VMEM((S, ROWS, N), bf16),
            pltpu.VMEM((len(OWN) * C, ROWS), f32),
            pltpu.VMEM((2, S * len(LEFT) * C, S * RIM), f32),
            pltpu.VMEM((len(OWN) * C, N), f32),
            pltpu.VMEM((S * len(LEFT) * C, N), f32),
            pltpu.VMEM((len(PAIRS), C, LANES), f32),
            pltpu.SemaphoreType.DMA((6,)),
            pltpu.SemaphoreType.DMA((CHUNKS,)),
            pltpu.SemaphoreType.DMA((2, CHUNKS)),
            pltpu.SemaphoreType.DMA((2, CHUNKS)),
            pltpu.SemaphoreType.DMA((2,)),
            pltpu.SemaphoreType.DMA((2,)),
        ],
        compiler_params=pltpu.CompilerParams(
            collective_id=0, has_side_effects=True, vmem_limit_bytes=56 << 20
        ),
        name="operator",
    )(forcing.reshape(S, ROWS, N), forcing.reshape(S, K, C, N), base_harm, mean_flow, mixing, harm_lo, couple_flags)


def solution(mesh):
    n_space, n_freq = mesh.shape["space"], mesh.shape["freq"]
    cells_all = S * K * n_freq * C * n_space * N // S
    y, xh, core, xl = 4, 2, 2, 2
    z = n_space // (xh * y)
    sizes = {"z": z, "xh": xh, "y": y, "xl": xl, "core": core}
    stages = [("z", "core"), ("xh", "xl", "y")]
    counts = []
    for axes in stages:
        count = 1
        for axis in axes:
            count *= sizes[axis]
        counts.append(count - 1)

    def gram_kernel(part_ref, gram_ref, mine, *rest):
        landing, send_sem, recv_sem = rest[:2], rest[2:4], rest[4:6]
        sp, fr = lax.axis_index("space"), lax.axis_index("freq")
        here = {
            "z": sp // (xh * y), "xh": sp // y % xh, "y": sp % y,
            "xl": fr // core, "core": fr % core,
        }

        def partner(axes, step):
            there = dict(here)
            for axis in axes:
                there[axis] = lax.rem(here[axis] + step % sizes[axis], sizes[axis])
                step //= sizes[axis]
            space = (there["z"] * xh + there["xh"]) * y + there["y"]
            return {"space": space, "freq": there["xl"] * core + there["core"]}

        barrier = pltpu.get_barrier_semaphore()
        for axes, count in zip(stages, counts):
            for step in range(1, count + 1):
                pl.semaphore_signal(
                    barrier, inc=1, device_id=partner(axes, step), device_id_type=MESH
                )
        pl.semaphore_wait(barrier, sum(counts))
        total = part_ref[...]
        for i, (axes, count) in enumerate(zip(stages, counts)):
            mine[i] = total
            copies = []
            for step in range(1, count + 1):
                copy = pltpu.make_async_remote_copy(
                    src_ref=mine.at[i],
                    dst_ref=landing[i].at[step - 1],
                    send_sem=send_sem[i].at[step - 1],
                    recv_sem=recv_sem[i].at[step - 1],
                    device_id=partner(axes, step),
                    device_id_type=MESH,
                )
                copy.start()
                copies.append(copy)
            for copy in copies:
                copy.wait_recv()
            total = total + jnp.sum(landing[i][...], axis=0)
            for copy in copies:
                copy.wait_send()
        gram_ref[...] = total[:S, :S] / cells_all

    def gram_sum(part):
        f32 = jnp.float32
        return pl.pallas_call(
            gram_kernel,
            out_shape=jax.ShapeDtypeStruct((S, S), f32),
            in_specs=[pl.BlockSpec(memory_space=pltpu.VMEM)],
            out_specs=pl.BlockSpec(memory_space=pltpu.VMEM),
            scratch_shapes=[pltpu.VMEM((2, C, 128), f32)]
            + [pltpu.VMEM((count, C, 128), f32) for count in counts]
            + [pltpu.SemaphoreType.DMA((count,)) for count in counts] * 2,
            compiler_params=pltpu.CompilerParams(collective_id=1, has_side_effects=True),
            name="gram_sum",
        )(part)

    def local(forcing, base_harm, mixing, mean_flow, harm_lo, couple_flags):
        shape = forcing.shape
        response, part = apply_operator(
            forcing,
            base_harm,
            mean_flow,
            mixing.transpose(1, 2, 0),
            harm_lo,
            couple_flags,
        )
        return response.reshape(shape), gram_sum(part)

    return jax.shard_map(
        local,
        mesh=mesh,
        in_specs=(
            P(None, "freq", None, "space", None),
            P(None, None, "space", None),
            P(),
            P(),
            P(),
            P("freq", None),
        ),
        out_specs=(P(None, "freq", None, "space", None), P()),
        check_vma=False,
    )
```

```python
import functools

import jax
import jax.numpy as jnp
from jax import lax
from jax.experimental import pallas as pl
from jax.experimental.pallas import tpu as pltpu
from jax.sharding import PartitionSpec as P

MESH = pl.DeviceIdType.MESH
S, K, C, N = 4, 8, 8, 1536
ROWS = K * C
NZ = 48
OMEGA = 0.05
VISCOSITY = 0.25
CHUNKS = 4
CROWS = ROWS // CHUNKS
RIM = 3 * C
Y = 4
DIRECT = 2
LANES = 256

OWN = [(j, k, k - j + 3) for k in range(K) for j in range(7) if 0 <= k - j + 3 < K]
LEFT = [(j, k, k - j + 6) for k in range(3) for j in range(7) if k - j + 3 < 0]
RIGHT = [(j, k, k - j + 3 - K) for k in range(K - 3, K) for j in range(7) if k - j + 3 >= K]

PAIRS = [(s, t) for s in range(S) for t in range(s, S)]


def split(coeff):
    high = coeff.astype(jnp.bfloat16)
    low = (coeff - high.astype(jnp.float32)).astype(jnp.bfloat16)
    return high, low


def swapped(value):
    return jnp.concatenate([value[4:], value[:4]], axis=0)


def pair_iota(width):
    row = lax.broadcasted_iota(jnp.int32, (C, width), 0)
    col = lax.broadcasted_iota(jnp.int32, (C, width), 1)
    return row, col


def mixing_tile(mix_ref, j, width):
    row, col = pair_iota(width)
    same = (row // 4) == ((col // 4) % 2)
    tile = jnp.zeros((C, width), jnp.float32)
    for v in range(4):
        for w in range(4):
            hit = same & (row % 4 == v) & (col % 4 == w)
            tile = jnp.where(hit, mix_ref[v, w, j], tile)
    return tile


def halo_kernel(
    f_ref, blocks_ref, base_ref, mean_ref, mix_hbm, lo_hbm, flag_hbm, resp_ref, part_ref,
    mix_ref, lo_ref, flag_ref,
    x_ref, from_left, from_right, rim_in, relay, base_in, mean_in, re_ref, im_ref,
    acc_ref, own_coeff, rim_coeff, mixed_ref, rim_mixed, gram_ref,
    in_sem, send_sem, recv_sem, rim_send, rim_recv, relay_sem,
):
    sp, fr = lax.axis_index("space"), lax.axis_index("freq")
    has_l, has_r = sp > 0, sp < lax.axis_size("space") - 1
    has_d, has_u = fr > 0, fr < lax.axis_size("freq") - 1
    to_l, to_r = {"space": sp - 1}, {"space": sp + 1}
    to_d, to_u = {"freq": fr - 1}, {"freq": fr + 1}
    edge = jnp.logical_or(sp % Y == 0, sp % Y == Y - 1)
    middle = jnp.logical_not(edge)
    up_hop, down_hop = fr == 1, fr == 2
    hop = jnp.logical_or(up_hop, down_hop)
    next_row = {"space": sp + 1 - 2 * (sp % 2)}
    across = {"space": sp + 1 - 2 * (sp % 2), "freq": 3 - fr}
    greeted = ((has_l, to_l), (has_r, to_r), (has_d, to_d), (has_u, to_u), (hop, across))

    barrier = pltpu.get_barrier_semaphore()
    for there, device in greeted:

        @pl.when(there)
        def _():
            pl.semaphore_signal(barrier, inc=1, device_id=device, device_id_type=MESH)

    load_x = pltpu.make_async_copy(f_ref, x_ref, in_sem.at[0])
    load_base = pltpu.make_async_copy(base_ref, base_in, in_sem.at[1])
    load_mean = pltpu.make_async_copy(mean_ref, mean_in, in_sem.at[2])
    loads = [load_x, load_base, load_mean]
    for i, (source, target) in enumerate(
        ((mix_hbm, mix_ref), (lo_hbm, lo_ref), (flag_hbm, flag_ref))
    ):
        loads.append(pltpu.make_async_copy(source, target, in_sem.at[3 + i]))
    for load in loads:
        load.start()
    peers = sum(there.astype(jnp.int32) for there, _ in greeted)
    pl.semaphore_wait(barrier, peers)

    def plane_copy(way, part):
        rows = pl.ds(part * CROWS, CROWS)
        landing = from_left if way == 0 else from_right
        return pltpu.make_async_remote_copy(
            src_ref=f_ref.at[:, rows],
            dst_ref=landing.at[:, rows],
            send_sem=send_sem.at[way, part],
            recv_sem=recv_sem.at[way, part],
            device_id=to_r if way == 0 else to_l,
            device_id_type=MESH,
        )

    def rim_of(way, low, high):
        first = K - 3 if way == 0 else 0
        return blocks_ref.at[low:high, first : first + 3]

    def rim_copy(way, low=0, high=S):
        return pltpu.make_async_remote_copy(
            src_ref=rim_of(way, low, high),
            dst_ref=rim_in.at[way, low:high],
            send_sem=rim_send.at[way],
            recv_sem=rim_recv.at[way],
            device_id=to_u if way == 0 else to_d,
            device_id_type=MESH,
        )

    def to_relay(way):
        return pltpu.make_async_remote_copy(
            src_ref=rim_of(way, DIRECT, S),
            dst_ref=relay,
            send_sem=relay_sem.at[0],
            recv_sem=relay_sem.at[1],
            device_id=next_row,
            device_id_type=MESH,
        )

    def from_relay(way):
        return pltpu.make_async_remote_copy(
            src_ref=relay,
            dst_ref=rim_in.at[way, DIRECT:],
            send_sem=relay_sem.at[2],
            recv_sem=relay_sem.at[3],
            device_id=across,
            device_id_type=MESH,
        )

    def when(*conditions):
        return pl.when(functools.reduce(jnp.logical_and, conditions))

    for way, there, far in ((0, has_u, up_hop), (1, has_d, down_hop)):
        split_up = jnp.logical_and(edge, far)

        @when(there, jnp.logical_not(split_up))
        def _():
            rim_copy(way).start()

        @when(split_up)
        def _():
            to_relay(way).start()
            rim_copy(way, 0, DIRECT).start()

    def start_planes(parts):
        for part in parts:
            for way, there in ((0, has_r), (1, has_l)):

                @when(there)
                def _():
                    plane_copy(way, part).start()

    start_planes(range(CHUNKS // 2))

    for way, there in ((0, has_d), (1, has_u)):

        @pl.when(jnp.logical_not(there))
        def _():
            rim_in[way] = jnp.zeros((S, 3, C, N), jnp.bfloat16)

    for landing, there in ((from_left, has_l), (from_right, has_r)):

        @pl.when(jnp.logical_not(there))
        def _():
            landing[...] = jnp.zeros((S, ROWS, N), jnp.bfloat16)

    for load in loads:
        load.wait()
    width = S * RIM
    row, col = pair_iota(width)
    for j in range(7):
        tile = mixing_tile(mix_ref, j, width)
        for slot, (jj, k, source) in enumerate(OWN):
            if jj == j:
                flag = flag_ref[k, j].astype(jnp.float32)
                block = jnp.where(col // C == source, tile, 0.0) * flag
                own_coeff[slot * C : slot * C + C, :] = block[:, :ROWS]
        for way, listed in ((0, LEFT), (1, RIGHT)):
            for slot, (jj, k, source) in enumerate(listed):
                if jj == j:
                    flag = flag_ref[k, j].astype(jnp.float32)
                    for s in range(S):
                        at = (s * len(listed) + slot) * C
                        block = jnp.where(col // C == 3 * s + source, tile, 0.0) * flag
                        rim_coeff[way, at : at + C, :] = block

    for j in range(7):
        re_ref[j] = jnp.broadcast_to(base_in[j, 0], (C, N))
        im_ref[j] = jnp.broadcast_to(base_in[j, 1], (C, N))

    @when(middle, hop)
    def _():
        to_relay(0).wait_recv()

    for way, far in ((0, up_hop), (1, down_hop)):

        @when(middle, far)
        def _():
            from_relay(way).start()

    start_planes(range(CHUNKS // 2, CHUNKS))

    own_high, own_low = split(own_coeff[...])
    own_both = jnp.concatenate([own_high, own_low], axis=1)
    sign = jnp.where(lax.broadcasted_iota(jnp.int32, (C, N), 0) < 4, 1.0, -1.0).astype(jnp.float32)
    first = lo_ref[0] + fr * K

    place = lax.broadcasted_iota(jnp.int32, (C, N), 1)
    span = place % NZ
    span_last, span_first = span == NZ - 1, span == 0
    wake_last, wake_first = place >= N - NZ, place < NZ

    def local_part(s, carry):
        values = x_ref[s]
        mixed_ref[...] = jnp.dot(
            own_both,
            jnp.concatenate([values, values], axis=0),
            preferred_element_type=jnp.float32,
        )
        for k in range(K):
            if k % 2 == 0:
                both = x_ref[s, k * C : k * C + 2 * C].astype(jnp.float32)
            x = both[(k % 2) * C : (k % 2) * C + C]
            up, down = pltpu.roll(x, N - 1, 1), pltpu.roll(x, 1, 1)
            span_up = jnp.where(span_last, pltpu.roll(x, NZ - 1, 1), up)
            span_down = jnp.where(span_first, pltpu.roll(x, N - NZ + 1, 1), down)
            wake_up = jnp.where(wake_last, 0.0, pltpu.roll(x, N - NZ, 1))
            wake_down = jnp.where(wake_first, 0.0, pltpu.roll(x, NZ, 1))
            around = VISCOSITY * (wake_up + wake_down + span_up + span_down - 6.0 * x)
            spin = OMEGA * (first + k).astype(jnp.float32)
            turned = spin * x
            straight = around
            for slot, (j, kk, _source) in enumerate(OWN):
                if kk == k:
                    mixed = mixed_ref[slot * C : slot * C + C, :]
                    straight = straight + re_ref[j] * mixed
                    turned = turned - im_ref[j] * mixed
            acc_ref[s, k * C : k * C + C] = swapped(sign * turned) - straight
        return carry

    lax.fori_loop(0, S, local_part, 0)

    for way, there, far, listed in ((0, has_d, down_hop, LEFT), (1, has_u, up_hop, RIGHT)):
        split_up = jnp.logical_and(edge, far)

        @when(there, jnp.logical_not(split_up))
        def _():
            rim_copy(way).wait_recv()

        @when(split_up)
        def _():
            rim_copy(way, 0, DIRECT).wait_recv()
            from_relay(way).wait_recv()

        high, low = split(rim_coeff[way])
        rim = rim_in[way].astype(jnp.float32).reshape(S * RIM, N).astype(jnp.bfloat16)
        rim_mixed[...] = jnp.dot(high, rim, preferred_element_type=jnp.float32) + jnp.dot(
            low, rim, preferred_element_type=jnp.float32
        )

        def rim_part(s, carry):
            for k in sorted({k for _, k, _ in listed}):
                straight = turned = None
                for slot, (j, kk, _source) in enumerate(listed):
                    if kk == k:
                        at = pl.multiple_of((s * len(listed) + slot) * C, C)
                        mixed = rim_mixed[pl.ds(at, C), :]
                        a, b = re_ref[j] * mixed, im_ref[j] * mixed
                        straight = a if straight is None else straight + a
                        turned = b if turned is None else turned + b
                acc_ref[s, k * C : k * C + C] -= swapped(sign * turned) + straight
            return carry

        lax.fori_loop(0, S, rim_part, 0)

    gram_ref[...] = jnp.zeros_like(gram_ref)
    half = 0.5 * mean_in[...].reshape(1, N)
    for part in range(CHUNKS):
        rows = slice(part * CROWS, (part + 1) * CROWS)
        for way, there in ((0, has_l), (1, has_r)):

            @pl.when(there)
            def _():
                plane_copy(way, part).wait_recv()

        sums = [gram_ref[p] for p in range(len(PAIRS))]
        for at in range(0, N, LANES):
            lanes = slice(at, at + LANES)
            gain_l = VISCOSITY + half[:, lanes]
            gain_r = VISCOSITY - half[:, lanes]
            rounded = []
            for s in range(S):
                left = from_left[s, rows, lanes].astype(jnp.float32)
                right = from_right[s, rows, lanes].astype(jnp.float32)
                value = acc_ref[s, rows, lanes] - (gain_l * left + gain_r * right)
                value = value.astype(jnp.bfloat16)
                resp_ref[s, rows, lanes] = value
                rounded.append(value.astype(jnp.float32))
            for p, (s, t) in enumerate(PAIRS):
                product = rounded[s] * rounded[t]
                sums[p] = sums[p] + (product[:C] + product[C:])
        for p in range(len(PAIRS)):
            gram_ref[p] = sums[p]

    row, col = pair_iota(128)
    tile = jnp.zeros((C, 128), jnp.float32)
    for p, (s, t) in enumerate(PAIRS):
        total = jnp.sum(gram_ref[p])
        hit = ((row == s) & (col == t)) | ((row == t) & (col == s))
        tile = jnp.where(hit, total, tile)
    part_ref[...] = tile

    for part in range(CHUNKS):
        for way, there in ((0, has_r), (1, has_l)):

            @pl.when(there)
            def _():
                plane_copy(way, part).wait_send()

    for way, there, far in ((0, has_u, up_hop), (1, has_d, down_hop)):
        split_up = jnp.logical_and(edge, far)

        @when(there, jnp.logical_not(split_up))
        def _():
            rim_copy(way).wait_send()

        @when(split_up)
        def _():
            rim_copy(way, 0, DIRECT).wait_send()
            to_relay(way).wait_send()

        @when(middle, far)
        def _():
            from_relay(way).wait_send()


def apply_operator(forcing, base_harm, mean_flow, mixing, harm_lo, couple_flags):
    hbm, vmem = pl.BlockSpec(memory_space=pltpu.HBM), pl.BlockSpec(memory_space=pltpu.VMEM)
    bf16, f32 = jnp.bfloat16, jnp.float32
    return pl.pallas_call(
        halo_kernel,
        out_shape=(
            pltpu.VMEM((S, ROWS, N), bf16),
            pltpu.VMEM((C, 128), f32),
        ),
        in_specs=[hbm] * 7,
        out_specs=(vmem, vmem),
        scratch_shapes=[
            pltpu.SMEM((4, 4, 7), f32),
            pltpu.SMEM((1,), jnp.int32),
            pltpu.SMEM((K, 7), jnp.int32),
            pltpu.VMEM((S, ROWS, N), bf16),
            pltpu.VMEM((S, ROWS, N), bf16),
            pltpu.VMEM((S, ROWS, N), bf16),
            pltpu.VMEM((2, S, 3, C, N), bf16),
            pltpu.VMEM((S - DIRECT, 3, C, N), bf16),
            pltpu.VMEM((7, 2, 1, N), f32),
            pltpu.VMEM((N,), f32),
            pltpu.VMEM((7, C, N), f32),
            pltpu.VMEM((7, C, N), f32),
            pltpu.VMEM((S, ROWS, N), f32),
            pltpu.VMEM((len(OWN) * C, ROWS), f32),
            pltpu.VMEM((2, S * len(LEFT) * C, S * RIM), f32),
            pltpu.VMEM((len(OWN) * C, N), f32),
            pltpu.VMEM((S * len(LEFT) * C, N), f32),
            pltpu.VMEM((len(PAIRS), C, LANES), f32),
            pltpu.SemaphoreType.DMA((6,)),
            pltpu.SemaphoreType.DMA((2, CHUNKS)),
            pltpu.SemaphoreType.DMA((2, CHUNKS)),
            pltpu.SemaphoreType.DMA((2,)),
            pltpu.SemaphoreType.DMA((2,)),
            pltpu.SemaphoreType.DMA((4,)),
        ],
        compiler_params=pltpu.CompilerParams(
            collective_id=0, has_side_effects=True, vmem_limit_bytes=62 << 20
        ),
        name="operator",
    )(forcing.reshape(S, ROWS, N), forcing.reshape(S, K, C, N), base_harm, mean_flow, mixing, harm_lo, couple_flags)


def solution(mesh):
    n_space, n_freq = mesh.shape["space"], mesh.shape["freq"]
    cells_all = S * K * n_freq * C * n_space * N // S
    y, xh, core, xl = 4, 2, 2, 2
    z = n_space // (xh * y)
    sizes = {"z": z, "xh": xh, "y": y, "xl": xl, "core": core}
    stages = [("z", "core"), ("xh", "xl", "y")]
    counts, orders = [], []

    def hops(axes, step):
        total = 0
        for axis in reversed(axes):
            by = step % sizes[axis]
            total += (2 if axis == "xh" else 1) * min(by, sizes[axis] - by)
            step //= sizes[axis]
        return total

    for axes in stages:
        count = 1
        for axis in axes:
            count *= sizes[axis]
        counts.append(count - 1)
        orders.append(sorted(range(1, count), key=lambda step: -hops(axes, step)))

    def gram_kernel(part_ref, gram_ref, mine, *rest):
        landing, send_sem, recv_sem = rest[:2], rest[2:4], rest[4:6]
        sp, fr = lax.axis_index("space"), lax.axis_index("freq")
        here = {
            "z": sp // (xh * y), "xh": sp // y % xh, "y": sp % y,
            "xl": fr // core, "core": fr % core,
        }

        def partner(axes, step):
            there = dict(here)
            for axis in reversed(axes):
                there[axis] = lax.rem(here[axis] + step % sizes[axis], sizes[axis])
                step //= sizes[axis]
            space = (there["z"] * xh + there["xh"]) * y + there["y"]
            return {"space": space, "freq": there["xl"] * core + there["core"]}

        barrier = pltpu.get_barrier_semaphore()
        for axes, order in zip(stages, orders):
            for step in order:
                pl.semaphore_signal(
                    barrier, inc=1, device_id=partner(axes, step), device_id_type=MESH
                )
        pl.semaphore_wait(barrier, sum(counts))
        total = part_ref[...]
        for i, (axes, order) in enumerate(zip(stages, orders)):
            mine[i] = total
            copies = []
            for step in order:
                copy = pltpu.make_async_remote_copy(
                    src_ref=mine.at[i],
                    dst_ref=landing[i].at[step - 1],
                    send_sem=send_sem[i].at[step - 1],
                    recv_sem=recv_sem[i].at[step - 1],
                    device_id=partner(axes, step),
                    device_id_type=MESH,
                )
                copy.start()
                copies.append(copy)
            for copy in copies:
                copy.wait_recv()
            total = total + jnp.sum(landing[i][...], axis=0)
            for copy in copies:
                copy.wait_send()
        gram_ref[...] = total

    def finish_kernel(resp_ref, total_ref, out_ref, gram_ref, sem):
        copy = pltpu.make_async_copy(resp_ref, out_ref, sem)
        copy.start()
        gram_ref[...] = total_ref[:S, :S] / cells_all
        copy.wait()

    def finish(response, total):
        return pl.pallas_call(
            finish_kernel,
            out_shape=(
                jax.ShapeDtypeStruct(response.shape, response.dtype),
                jax.ShapeDtypeStruct((S, S), jnp.float32),
            ),
            in_specs=[
                pl.BlockSpec(memory_space=pl.ANY),
                pl.BlockSpec(memory_space=pltpu.VMEM),
            ],
            out_specs=(
                pl.BlockSpec(memory_space=pltpu.HBM),
                pl.BlockSpec(memory_space=pltpu.VMEM),
            ),
            scratch_shapes=[pltpu.SemaphoreType.DMA],
            compiler_params=pltpu.CompilerParams(vmem_limit_bytes=4 << 20),
            name="finish",
        )(response, total)

    def gram_sum(part):
        f32 = jnp.float32
        return pl.pallas_call(
            gram_kernel,
            out_shape=pltpu.VMEM((C, 128), f32),
            in_specs=[pl.BlockSpec(memory_space=pltpu.VMEM)],
            out_specs=pl.BlockSpec(memory_space=pltpu.VMEM),
            scratch_shapes=[pltpu.VMEM((2, C, 128), f32)]
            + [pltpu.VMEM((count, C, 128), f32) for count in counts]
            + [pltpu.SemaphoreType.DMA((count,)) for count in counts] * 2,
            compiler_params=pltpu.CompilerParams(
                collective_id=1, has_side_effects=True, vmem_limit_bytes=4 << 20
            ),
            name="gram_sum",
        )(part)

    def local(forcing, base_harm, mixing, mean_flow, harm_lo, couple_flags):
        shape = forcing.shape
        response, part = apply_operator(
            forcing,
            base_harm,
            mean_flow,
            mixing.transpose(1, 2, 0),
            harm_lo,
            couple_flags,
        )
        response, gram_matrix = finish(response, gram_sum(part))
        return response.reshape(shape), gram_matrix

    return jax.shard_map(
        local,
        mesh=mesh,
        in_specs=(
            P(None, "freq", None, "space", None),
            P(None, None, "space", None),
            P(),
            P(),
            P(),
            P("freq", None),
        ),
        out_specs=(P(None, "freq", None, "space", None), P()),
        check_vma=False,
    )
```

```python
import functools

import jax
import jax.numpy as jnp
from jax import lax
from jax.experimental import pallas as pl
from jax.experimental.pallas import tpu as pltpu
from jax.sharding import PartitionSpec as P

MESH = pl.DeviceIdType.MESH
S, K, C, N = 4, 8, 8, 1536
ROWS = K * C
NZ = 48
OMEGA = 0.05
VISCOSITY = 0.25
CHUNKS = 4
CROWS = ROWS // CHUNKS
RIM = 3 * C
Y = 4
DIRECT = 1
LANES = 256

OWN = [(j, k, k - j + 3) for k in range(K) for j in range(7) if 0 <= k - j + 3 < K]
LEFT = [(j, k, k - j + 6) for k in range(3) for j in range(7) if k - j + 3 < 0]
RIGHT = [(j, k, k - j + 3 - K) for k in range(K - 3, K) for j in range(7) if k - j + 3 >= K]

PAIRS = [(s, t) for s in range(S) for t in range(s, S)]


def split(coeff):
    high = coeff.astype(jnp.bfloat16)
    low = (coeff - high.astype(jnp.float32)).astype(jnp.bfloat16)
    return high, low


def swapped(value):
    return jnp.concatenate([value[4:], value[:4]], axis=0)


def pair_iota(width):
    row = lax.broadcasted_iota(jnp.int32, (C, width), 0)
    col = lax.broadcasted_iota(jnp.int32, (C, width), 1)
    return row, col


def mixing_tile(mix_ref, j, width):
    row, col = pair_iota(width)
    same = (row // 4) == ((col // 4) % 2)
    tile = jnp.zeros((C, width), jnp.float32)
    for v in range(4):
        for w in range(4):
            hit = same & (row % 4 == v) & (col % 4 == w)
            tile = jnp.where(hit, mix_ref[v, w, j], tile)
    return tile


def halo_kernel(
    f_ref, blocks_ref, base_ref, mean_ref, mix_hbm, lo_hbm, flag_hbm, resp_ref, part_ref,
    mix_ref, lo_ref, flag_ref,
    x_ref, from_left, from_right, rim_in, relay, base_in, mean_in, re_ref, im_ref,
    acc_ref, own_coeff, rim_coeff, mixed_ref, rim_mixed, gram_ref,
    in_sem, send_sem, recv_sem, rim_send, rim_recv, relay_sem,
):
    sp, fr = lax.axis_index("space"), lax.axis_index("freq")
    has_l, has_r = sp > 0, sp < lax.axis_size("space") - 1
    has_d, has_u = fr > 0, fr < lax.axis_size("freq") - 1
    to_l, to_r = {"space": sp - 1}, {"space": sp + 1}
    to_d, to_u = {"freq": fr - 1}, {"freq": fr + 1}
    edge = jnp.logical_or(sp % Y == 0, sp % Y == Y - 1)
    middle = jnp.logical_not(edge)
    up_hop, down_hop = fr == 1, fr == 2
    hop = jnp.logical_or(up_hop, down_hop)
    next_row = {"space": sp + 1 - 2 * (sp % 2)}
    across = {"space": sp + 1 - 2 * (sp % 2), "freq": 3 - fr}
    greeted = ((has_l, to_l), (has_r, to_r), (has_d, to_d), (has_u, to_u), (hop, across))

    barrier = pltpu.get_barrier_semaphore()
    for there, device in greeted:

        @pl.when(there)
        def _():
            pl.semaphore_signal(barrier, inc=1, device_id=device, device_id_type=MESH)

    load_x = pltpu.make_async_copy(f_ref, x_ref, in_sem.at[0])
    load_base = pltpu.make_async_copy(base_ref, base_in, in_sem.at[1])
    load_mean = pltpu.make_async_copy(mean_ref, mean_in, in_sem.at[2])
    loads = [load_x, load_base, load_mean]
    for i, (source, target) in enumerate(
        ((mix_hbm, mix_ref), (lo_hbm, lo_ref), (flag_hbm, flag_ref))
    ):
        loads.append(pltpu.make_async_copy(source, target, in_sem.at[3 + i]))
    for load in loads:
        load.start()
    peers = sum(there.astype(jnp.int32) for there, _ in greeted)
    pl.semaphore_wait(barrier, peers)

    def plane_copy(way, part):
        rows = pl.ds(part * CROWS, CROWS)
        landing = from_left if way == 0 else from_right
        return pltpu.make_async_remote_copy(
            src_ref=f_ref.at[:, rows],
            dst_ref=landing.at[:, rows],
            send_sem=send_sem.at[way, part],
            recv_sem=recv_sem.at[way, part],
            device_id=to_r if way == 0 else to_l,
            device_id_type=MESH,
        )

    def rim_of(way, low, high):
        first = K - 3 if way == 0 else 0
        return blocks_ref.at[low:high, first : first + 3]

    def rim_copy(way, low=0, high=S):
        return pltpu.make_async_remote_copy(
            src_ref=rim_of(way, low, high),
            dst_ref=rim_in.at[way, low:high],
            send_sem=rim_send.at[way],
            recv_sem=rim_recv.at[way],
            device_id=to_u if way == 0 else to_d,
            device_id_type=MESH,
        )

    def to_relay(way):
        return pltpu.make_async_remote_copy(
            src_ref=rim_of(way, DIRECT, S),
            dst_ref=relay,
            send_sem=relay_sem.at[0],
            recv_sem=relay_sem.at[1],
            device_id=next_row,
            device_id_type=MESH,
        )

    def from_relay(way):
        return pltpu.make_async_remote_copy(
            src_ref=relay,
            dst_ref=rim_in.at[way, DIRECT:],
            send_sem=relay_sem.at[2],
            recv_sem=relay_sem.at[3],
            device_id=across,
            device_id_type=MESH,
        )

    def when(*conditions):
        return pl.when(functools.reduce(jnp.logical_and, conditions))

    for way, there, far in ((0, has_u, up_hop), (1, has_d, down_hop)):
        split_up = jnp.logical_and(edge, far)

        @when(there, jnp.logical_not(split_up))
        def _():
            rim_copy(way).start()

        @when(split_up)
        def _():
            to_relay(way).start()
            rim_copy(way, 0, DIRECT).start()

    def start_planes(parts):
        for part in parts:
            for way, there in ((0, has_r), (1, has_l)):

                @when(there)
                def _():
                    plane_copy(way, part).start()

    start_planes(range(CHUNKS // 2))

    @when(middle, hop)
    def _():
        to_relay(0).wait_recv()

    for way, far in ((0, up_hop), (1, down_hop)):

        @when(middle, far)
        def _():
            from_relay(way).start()

    start_planes(range(CHUNKS // 2, CHUNKS))

    for way, there in ((0, has_d), (1, has_u)):

        @pl.when(jnp.logical_not(there))
        def _():
            rim_in[way] = jnp.zeros((S, 3, C, N), jnp.bfloat16)

    for landing, there in ((from_left, has_l), (from_right, has_r)):

        @pl.when(jnp.logical_not(there))
        def _():
            landing[...] = jnp.zeros((S, ROWS, N), jnp.bfloat16)

    for load in loads:
        load.wait()
    width = S * RIM
    row, col = pair_iota(width)
    for j in range(7):
        tile = mixing_tile(mix_ref, j, width)
        for slot, (jj, k, source) in enumerate(OWN):
            if jj == j:
                flag = flag_ref[k, j].astype(jnp.float32)
                block = jnp.where(col // C == source, tile, 0.0) * flag
                own_coeff[slot * C : slot * C + C, :] = block[:, :ROWS]
        for way, listed in ((0, LEFT), (1, RIGHT)):
            for slot, (jj, k, source) in enumerate(listed):
                if jj == j:
                    flag = flag_ref[k, j].astype(jnp.float32)
                    for s in range(S):
                        at = (s * len(listed) + slot) * C
                        block = jnp.where(col // C == 3 * s + source, tile, 0.0) * flag
                        rim_coeff[way, at : at + C, :] = block

    for j in range(7):
        re_ref[j] = jnp.broadcast_to(base_in[j, 0], (C, N))
        im_ref[j] = jnp.broadcast_to(base_in[j, 1], (C, N))

    own_high, own_low = split(own_coeff[...])
    own_both = jnp.concatenate([own_high, own_low], axis=1)
    sign = jnp.where(lax.broadcasted_iota(jnp.int32, (C, N), 0) < 4, 1.0, -1.0).astype(jnp.float32)
    first = lo_ref[0] + fr * K

    place = lax.broadcasted_iota(jnp.int32, (C, N), 1)
    span = place % NZ
    span_last, span_first = span == NZ - 1, span == 0
    wake_last, wake_first = place >= N - NZ, place < NZ

    def local_part(s, carry):
        values = x_ref[s]
        mixed_ref[...] = jnp.dot(
            own_both,
            jnp.concatenate([values, values], axis=0),
            preferred_element_type=jnp.float32,
        )
        for k in range(K):
            if k % 2 == 0:
                both = x_ref[s, k * C : k * C + 2 * C].astype(jnp.float32)
            x = both[(k % 2) * C : (k % 2) * C + C]
            up, down = pltpu.roll(x, N - 1, 1), pltpu.roll(x, 1, 1)
            span_up = jnp.where(span_last, pltpu.roll(x, NZ - 1, 1), up)
            span_down = jnp.where(span_first, pltpu.roll(x, N - NZ + 1, 1), down)
            wake_up = jnp.where(wake_last, 0.0, pltpu.roll(x, N - NZ, 1))
            wake_down = jnp.where(wake_first, 0.0, pltpu.roll(x, NZ, 1))
            around = VISCOSITY * (wake_up + wake_down + span_up + span_down - 6.0 * x)
            spin = OMEGA * (first + k).astype(jnp.float32)
            turned = spin * x
            straight = around
            for slot, (j, kk, _source) in enumerate(OWN):
                if kk == k:
                    mixed = mixed_ref[slot * C : slot * C + C, :]
                    straight = straight + re_ref[j] * mixed
                    turned = turned - im_ref[j] * mixed
            acc_ref[s, k * C : k * C + C] = swapped(sign * turned) - straight
        return carry

    lax.fori_loop(0, S, local_part, 0)

    for way, there, far, listed in ((0, has_d, down_hop, LEFT), (1, has_u, up_hop, RIGHT)):
        split_up = jnp.logical_and(edge, far)

        @when(there, jnp.logical_not(split_up))
        def _():
            rim_copy(way).wait_recv()

        @when(split_up)
        def _():
            rim_copy(way, 0, DIRECT).wait_recv()
            from_relay(way).wait_recv()

        high, low = split(rim_coeff[way])
        rim = rim_in[way].astype(jnp.float32).reshape(S * RIM, N).astype(jnp.bfloat16)
        rim_mixed[...] = jnp.dot(high, rim, preferred_element_type=jnp.float32) + jnp.dot(
            low, rim, preferred_element_type=jnp.float32
        )

        def rim_part(s, carry):
            for k in sorted({k for _, k, _ in listed}):
                straight = turned = None
                for slot, (j, kk, _source) in enumerate(listed):
                    if kk == k:
                        at = pl.multiple_of((s * len(listed) + slot) * C, C)
                        mixed = rim_mixed[pl.ds(at, C), :]
                        a, b = re_ref[j] * mixed, im_ref[j] * mixed
                        straight = a if straight is None else straight + a
                        turned = b if turned is None else turned + b
                acc_ref[s, k * C : k * C + C] -= swapped(sign * turned) + straight
            return carry

        lax.fori_loop(0, S, rim_part, 0)

    gram_ref[...] = jnp.zeros_like(gram_ref)
    half = 0.5 * mean_in[...].reshape(1, N)
    for part in range(CHUNKS):
        rows = slice(part * CROWS, (part + 1) * CROWS)
        for way, there in ((0, has_l), (1, has_r)):

            @pl.when(there)
            def _():
                plane_copy(way, part).wait_recv()

        sums = [gram_ref[p] for p in range(len(PAIRS))]
        for at in range(0, N, LANES):
            lanes = slice(at, at + LANES)
            gain_l = VISCOSITY + half[:, lanes]
            gain_r = VISCOSITY - half[:, lanes]
            rounded = []
            for s in range(S):
                left = from_left[s, rows, lanes].astype(jnp.float32)
                right = from_right[s, rows, lanes].astype(jnp.float32)
                value = acc_ref[s, rows, lanes] - (gain_l * left + gain_r * right)
                value = value.astype(jnp.bfloat16)
                resp_ref[s, rows, lanes] = value
                rounded.append(value.astype(jnp.float32))
            for p, (s, t) in enumerate(PAIRS):
                product = rounded[s] * rounded[t]
                sums[p] = sums[p] + (product[:C] + product[C:])
        for p in range(len(PAIRS)):
            gram_ref[p] = sums[p]

    row, col = pair_iota(128)
    tile = jnp.zeros((C, 128), jnp.float32)
    for p, (s, t) in enumerate(PAIRS):
        total = jnp.sum(gram_ref[p])
        hit = ((row == s) & (col == t)) | ((row == t) & (col == s))
        tile = jnp.where(hit, total, tile)
    part_ref[...] = tile

    for part in range(CHUNKS):
        for way, there in ((0, has_r), (1, has_l)):

            @pl.when(there)
            def _():
                plane_copy(way, part).wait_send()

    for way, there, far in ((0, has_u, up_hop), (1, has_d, down_hop)):
        split_up = jnp.logical_and(edge, far)

        @when(there, jnp.logical_not(split_up))
        def _():
            rim_copy(way).wait_send()

        @when(split_up)
        def _():
            rim_copy(way, 0, DIRECT).wait_send()
            to_relay(way).wait_send()

        @when(middle, far)
        def _():
            from_relay(way).wait_send()


def apply_operator(forcing, base_harm, mean_flow, mixing, harm_lo, couple_flags):
    hbm, vmem = pl.BlockSpec(memory_space=pltpu.HBM), pl.BlockSpec(memory_space=pltpu.VMEM)
    bf16, f32 = jnp.bfloat16, jnp.float32
    return pl.pallas_call(
        halo_kernel,
        out_shape=(
            pltpu.VMEM((S, ROWS, N), bf16),
            pltpu.VMEM((C, 128), f32),
        ),
        in_specs=[hbm] * 7,
        out_specs=(vmem, vmem),
        scratch_shapes=[
            pltpu.SMEM((4, 4, 7), f32),
            pltpu.SMEM((1,), jnp.int32),
            pltpu.SMEM((K, 7), jnp.int32),
            pltpu.VMEM((S, ROWS, N), bf16),
            pltpu.VMEM((S, ROWS, N), bf16),
            pltpu.VMEM((S, ROWS, N), bf16),
            pltpu.VMEM((2, S, 3, C, N), bf16),
            pltpu.VMEM((S - DIRECT, 3, C, N), bf16),
            pltpu.VMEM((7, 2, 1, N), f32),
            pltpu.VMEM((N,), f32),
            pltpu.VMEM((7, C, N), f32),
            pltpu.VMEM((7, C, N), f32),
            pltpu.VMEM((S, ROWS, N), f32),
            pltpu.VMEM((len(OWN) * C, ROWS), f32),
            pltpu.VMEM((2, S * len(LEFT) * C, S * RIM), f32),
            pltpu.VMEM((len(OWN) * C, N), f32),
            pltpu.VMEM((S * len(LEFT) * C, N), f32),
            pltpu.VMEM((len(PAIRS), C, LANES), f32),
            pltpu.SemaphoreType.DMA((6,)),
            pltpu.SemaphoreType.DMA((2, CHUNKS)),
            pltpu.SemaphoreType.DMA((2, CHUNKS)),
            pltpu.SemaphoreType.DMA((2,)),
            pltpu.SemaphoreType.DMA((2,)),
            pltpu.SemaphoreType.DMA((4,)),
        ],
        compiler_params=pltpu.CompilerParams(
            collective_id=0, has_side_effects=True, vmem_limit_bytes=62 << 20
        ),
        name="operator",
    )(forcing.reshape(S, ROWS, N), forcing.reshape(S, K, C, N), base_harm, mean_flow, mixing, harm_lo, couple_flags)


def solution(mesh):
    n_space, n_freq = mesh.shape["space"], mesh.shape["freq"]
    cells_all = S * K * n_freq * C * n_space * N // S
    y, xh, core, xl = 4, 2, 2, 2
    z = n_space // (xh * y)
    sizes = {"z": z, "xh": xh, "y": y, "xl": xl, "core": core}
    stages = [("z", "core"), ("xh", "xl", "y")]
    counts, orders = [], []

    def hops(axes, step):
        total = 0
        for axis in reversed(axes):
            by = step % sizes[axis]
            total += (2 if axis == "xh" else 1) * min(by, sizes[axis] - by)
            step //= sizes[axis]
        return total

    for axes in stages:
        count = 1
        for axis in axes:
            count *= sizes[axis]
        counts.append(count - 1)
        orders.append(sorted(range(1, count), key=lambda step: -hops(axes, step)))

    def gram_kernel(part_ref, gram_ref, mine, *rest):
        landing, send_sem, recv_sem = rest[:2], rest[2:4], rest[4:6]
        sp, fr = lax.axis_index("space"), lax.axis_index("freq")
        here = {
            "z": sp // (xh * y), "xh": sp // y % xh, "y": sp % y,
            "xl": fr // core, "core": fr % core,
        }

        def partner(axes, step):
            there = dict(here)
            for axis in reversed(axes):
                there[axis] = lax.rem(here[axis] + step % sizes[axis], sizes[axis])
                step //= sizes[axis]
            space = (there["z"] * xh + there["xh"]) * y + there["y"]
            return {"space": space, "freq": there["xl"] * core + there["core"]}

        barrier = pltpu.get_barrier_semaphore()
        for axes, order in zip(stages, orders):
            for step in order:
                pl.semaphore_signal(
                    barrier, inc=1, device_id=partner(axes, step), device_id_type=MESH
                )
        pl.semaphore_wait(barrier, sum(counts))
        total = part_ref[...]
        for i, (axes, order) in enumerate(zip(stages, orders)):
            mine[i] = total
            copies = []
            for step in order:
                copy = pltpu.make_async_remote_copy(
                    src_ref=mine.at[i],
                    dst_ref=landing[i].at[step - 1],
                    send_sem=send_sem[i].at[step - 1],
                    recv_sem=recv_sem[i].at[step - 1],
                    device_id=partner(axes, step),
                    device_id_type=MESH,
                )
                copy.start()
                copies.append(copy)
            for copy in copies:
                copy.wait_recv()
            total = total + jnp.sum(landing[i][...], axis=0)
            for copy in copies:
                copy.wait_send()
        gram_ref[...] = total

    def finish_kernel(resp_ref, total_ref, out_ref, gram_ref, gram_here, sem):
        copies = [
            pltpu.make_async_copy(resp_ref.at[s], out_ref.at[s], sem.at[s]) for s in range(S)
        ]
        for copy in copies:
            copy.start()
        gram_here[...] = total_ref[:S, :S] / cells_all
        copies.append(pltpu.make_async_copy(gram_here, gram_ref, sem.at[S]))
        copies[S].start()
        for copy in copies:
            copy.wait()

    def finish(response, total):
        return pl.pallas_call(
            finish_kernel,
            out_shape=(
                jax.ShapeDtypeStruct(response.shape, response.dtype),
                jax.ShapeDtypeStruct((S, S), jnp.float32),
            ),
            in_specs=[
                pl.BlockSpec(memory_space=pl.ANY),
                pl.BlockSpec(memory_space=pltpu.VMEM),
            ],
            out_specs=(
                pl.BlockSpec(memory_space=pltpu.HBM),
                pl.BlockSpec(memory_space=pltpu.HBM),
            ),
            scratch_shapes=[
                pltpu.VMEM((S, S), jnp.float32),
                pltpu.SemaphoreType.DMA((S + 1,)),
            ],
            compiler_params=pltpu.CompilerParams(vmem_limit_bytes=4 << 20),
            name="finish",
        )(response, total)

    def gram_sum(part):
        f32 = jnp.float32
        return pl.pallas_call(
            gram_kernel,
            out_shape=pltpu.VMEM((C, 128), f32),
            in_specs=[pl.BlockSpec(memory_space=pltpu.VMEM)],
            out_specs=pl.BlockSpec(memory_space=pltpu.VMEM),
            scratch_shapes=[pltpu.VMEM((2, C, 128), f32)]
            + [pltpu.VMEM((count, C, 128), f32) for count in counts]
            + [pltpu.SemaphoreType.DMA((count,)) for count in counts] * 2,
            compiler_params=pltpu.CompilerParams(
                collective_id=1, has_side_effects=True, vmem_limit_bytes=4 << 20
            ),
            name="gram_sum",
        )(part)

    def local(forcing, base_harm, mixing, mean_flow, harm_lo, couple_flags):
        shape = forcing.shape
        response, part = apply_operator(
            forcing,
            base_harm,
            mean_flow,
            mixing.transpose(1, 2, 0),
            harm_lo,
            couple_flags,
        )
        response, gram_matrix = finish(response, gram_sum(part))
        return response.reshape(shape), gram_matrix

    return jax.shard_map(
        local,
        mesh=mesh,
        in_specs=(
            P(None, "freq", None, "space", None),
            P(None, None, "space", None),
            P(),
            P(),
            P(),
            P("freq", None),
        ),
        out_specs=(P(None, "freq", None, "space", None), P()),
        check_vma=False,
    )
```

```python
import functools

import jax
import jax.numpy as jnp
from jax import lax
from jax.experimental import pallas as pl
from jax.experimental.pallas import tpu as pltpu
from jax.sharding import PartitionSpec as P

MESH = pl.DeviceIdType.MESH
S, K, C, N = 4, 8, 8, 1536
ROWS = K * C
NZ = 48
OMEGA = 0.05
VISCOSITY = 0.25
CHUNKS = 4
CROWS = ROWS // CHUNKS
RIM = 3 * C
Y = 4
DIRECT = 1
LANES = 256

OWN = [(j, k, k - j + 3) for k in range(K) for j in range(7) if 0 <= k - j + 3 < K]
LEFT = [(j, k, k - j + 6) for k in range(3) for j in range(7) if k - j + 3 < 0]
RIGHT = [(j, k, k - j + 3 - K) for k in range(K - 3, K) for j in range(7) if k - j + 3 >= K]

PAIRS = [(s, t) for s in range(S) for t in range(s, S)]


def split(coeff):
    high = coeff.astype(jnp.bfloat16)
    low = (coeff - high.astype(jnp.float32)).astype(jnp.bfloat16)
    return high, low


def swapped(value):
    return jnp.concatenate([value[4:], value[:4]], axis=0)


def pair_iota(width):
    row = lax.broadcasted_iota(jnp.int32, (C, width), 0)
    col = lax.broadcasted_iota(jnp.int32, (C, width), 1)
    return row, col


def mixing_tile(mix_ref, j, width):
    row, col = pair_iota(width)
    same = (row // 4) == ((col // 4) % 2)
    tile = jnp.zeros((C, width), jnp.float32)
    for v in range(4):
        for w in range(4):
            hit = same & (row % 4 == v) & (col % 4 == w)
            tile = jnp.where(hit, mix_ref[v, w, j], tile)
    return tile


def halo_kernel(
    f_ref, blocks_ref, base_ref, mean_ref, mix_hbm, lo_hbm, flag_hbm, resp_ref, part_ref,
    mix_ref, lo_ref, flag_ref,
    x_ref, from_left, from_right, rim_in, relay, base_in, mean_in, re_ref, im_ref,
    acc_ref, own_coeff, rim_coeff, mixed_ref, rim_mixed, gram_ref,
    in_sem, send_sem, recv_sem, rim_send, rim_recv, relay_sem,
):
    sp, fr = lax.axis_index("space"), lax.axis_index("freq")
    has_l, has_r = sp > 0, sp < lax.axis_size("space") - 1
    has_d, has_u = fr > 0, fr < lax.axis_size("freq") - 1
    to_l, to_r = {"space": sp - 1}, {"space": sp + 1}
    to_d, to_u = {"freq": fr - 1}, {"freq": fr + 1}
    edge = jnp.logical_or(sp % Y == 0, sp % Y == Y - 1)
    middle = jnp.logical_not(edge)
    up_hop, down_hop = fr == 1, fr == 2
    hop = jnp.logical_or(up_hop, down_hop)
    next_row = {"space": sp + 1 - 2 * (sp % 2)}
    across = {"space": sp + 1 - 2 * (sp % 2), "freq": 3 - fr}
    greeted = ((has_l, to_l), (has_r, to_r), (has_d, to_d), (has_u, to_u), (hop, across))

    barrier = pltpu.get_barrier_semaphore()
    for there, device in greeted:

        @pl.when(there)
        def _():
            pl.semaphore_signal(barrier, inc=1, device_id=device, device_id_type=MESH)

    load_x = pltpu.make_async_copy(f_ref, x_ref, in_sem.at[0])
    load_base = pltpu.make_async_copy(base_ref, base_in, in_sem.at[1])
    load_mean = pltpu.make_async_copy(mean_ref, mean_in, in_sem.at[2])
    loads = [load_x, load_base, load_mean]
    for i, (source, target) in enumerate(
        ((mix_hbm, mix_ref), (lo_hbm, lo_ref), (flag_hbm, flag_ref))
    ):
        loads.append(pltpu.make_async_copy(source, target, in_sem.at[3 + i]))
    for load in loads:
        load.start()
    peers = sum(there.astype(jnp.int32) for there, _ in greeted)
    pl.semaphore_wait(barrier, peers)

    def plane_copy(way, part):
        rows = pl.ds(part * CROWS, CROWS)
        landing = from_left if way == 0 else from_right
        return pltpu.make_async_remote_copy(
            src_ref=f_ref.at[:, rows],
            dst_ref=landing.at[:, rows],
            send_sem=send_sem.at[way, part],
            recv_sem=recv_sem.at[way, part],
            device_id=to_r if way == 0 else to_l,
            device_id_type=MESH,
        )

    def rim_of(way, low, high):
        first = K - 3 if way == 0 else 0
        return blocks_ref.at[low:high, first : first + 3]

    def rim_copy(way, low=0, high=S):
        return pltpu.make_async_remote_copy(
            src_ref=rim_of(way, low, high),
            dst_ref=rim_in.at[way, low:high],
            send_sem=rim_send.at[way],
            recv_sem=rim_recv.at[way],
            device_id=to_u if way == 0 else to_d,
            device_id_type=MESH,
        )

    def to_relay(way):
        return pltpu.make_async_remote_copy(
            src_ref=rim_of(way, DIRECT, S),
            dst_ref=relay,
            send_sem=relay_sem.at[0],
            recv_sem=relay_sem.at[1],
            device_id=next_row,
            device_id_type=MESH,
        )

    def from_relay(way):
        return pltpu.make_async_remote_copy(
            src_ref=relay,
            dst_ref=rim_in.at[way, DIRECT:],
            send_sem=relay_sem.at[2],
            recv_sem=relay_sem.at[3],
            device_id=across,
            device_id_type=MESH,
        )

    def when(*conditions):
        return pl.when(functools.reduce(jnp.logical_and, conditions))

    for way, there, far in ((0, has_u, up_hop), (1, has_d, down_hop)):
        split_up = jnp.logical_and(edge, far)

        @when(there, jnp.logical_not(split_up))
        def _():
            rim_copy(way).start()

        @when(split_up)
        def _():
            to_relay(way).start()
            rim_copy(way, 0, DIRECT).start()

    def start_planes(parts):
        for part in parts:
            for way, there in ((0, has_r), (1, has_l)):

                @when(there)
                def _():
                    plane_copy(way, part).start()

    start_planes(range(CHUNKS // 2))

    @when(middle, hop)
    def _():
        to_relay(0).wait_recv()

    for way, far in ((0, up_hop), (1, down_hop)):

        @when(middle, far)
        def _():
            from_relay(way).start()

    start_planes(range(CHUNKS // 2, CHUNKS))

    for way, there in ((0, has_d), (1, has_u)):

        @pl.when(jnp.logical_not(there))
        def _():
            rim_in[way] = jnp.zeros((S, 3, C, N), jnp.bfloat16)

    for landing, there in ((from_left, has_l), (from_right, has_r)):

        @pl.when(jnp.logical_not(there))
        def _():
            landing[...] = jnp.zeros((S, ROWS, N), jnp.bfloat16)

    for load in loads:
        load.wait()
    width = S * RIM
    row, col = pair_iota(width)
    for j in range(7):
        tile = mixing_tile(mix_ref, j, width)
        for slot, (jj, k, source) in enumerate(OWN):
            if jj == j:
                flag = flag_ref[k, j].astype(jnp.float32)
                block = jnp.where(col // C == source, tile, 0.0) * flag
                own_coeff[slot * C : slot * C + C, :] = block[:, :ROWS]
        for way, listed in ((0, LEFT), (1, RIGHT)):
            for slot, (jj, k, source) in enumerate(listed):
                if jj == j:
                    flag = flag_ref[k, j].astype(jnp.float32)
                    for s in range(S):
                        at = (s * len(listed) + slot) * C
                        block = jnp.where(col // C == 3 * s + source, tile, 0.0) * flag
                        rim_coeff[way, at : at + C, :] = block

    for j in range(7):
        re_ref[j] = jnp.broadcast_to(base_in[j, 0], (C, N))
        im_ref[j] = jnp.broadcast_to(base_in[j, 1], (C, N))

    own_high, own_low = split(own_coeff[...])
    own_both = jnp.concatenate([own_high, own_low], axis=1)
    sign = jnp.where(lax.broadcasted_iota(jnp.int32, (C, N), 0) < 4, 1.0, -1.0).astype(jnp.float32)
    first = lo_ref[0] + fr * K

    place = lax.broadcasted_iota(jnp.int32, (C, N), 1)
    span = place % NZ
    span_last, span_first = span == NZ - 1, span == 0
    wake_last, wake_first = place >= N - NZ, place < NZ

    def local_part(s, carry):
        values = x_ref[s]
        mixed_ref[...] = jnp.dot(
            own_both,
            jnp.concatenate([values, values], axis=0),
            preferred_element_type=jnp.float32,
        )
        for k in range(K):
            if k % 2 == 0:
                both = x_ref[s, k * C : k * C + 2 * C].astype(jnp.float32)
            x = both[(k % 2) * C : (k % 2) * C + C]
            up, down = pltpu.roll(x, N - 1, 1), pltpu.roll(x, 1, 1)
            span_up = jnp.where(span_last, pltpu.roll(x, NZ - 1, 1), up)
            span_down = jnp.where(span_first, pltpu.roll(x, N - NZ + 1, 1), down)
            wake_up = jnp.where(wake_last, 0.0, pltpu.roll(x, N - NZ, 1))
            wake_down = jnp.where(wake_first, 0.0, pltpu.roll(x, NZ, 1))
            around = VISCOSITY * (wake_up + wake_down + span_up + span_down - 6.0 * x)
            spin = OMEGA * (first + k).astype(jnp.float32)
            turned = spin * x
            straight = around
            for slot, (j, kk, _source) in enumerate(OWN):
                if kk == k:
                    mixed = mixed_ref[slot * C : slot * C + C, :]
                    straight = straight + re_ref[j] * mixed
                    turned = turned - im_ref[j] * mixed
            acc_ref[s, k * C : k * C + C] = swapped(sign * turned) - straight
        return carry

    lax.fori_loop(0, S, local_part, 0)

    for way, there, far, listed in ((0, has_d, down_hop, LEFT), (1, has_u, up_hop, RIGHT)):
        split_up = jnp.logical_and(edge, far)

        @when(there, jnp.logical_not(split_up))
        def _():
            rim_copy(way).wait_recv()

        @when(split_up)
        def _():
            rim_copy(way, 0, DIRECT).wait_recv()
            from_relay(way).wait_recv()

        high, low = split(rim_coeff[way])
        rim = rim_in[way].astype(jnp.float32).reshape(S * RIM, N).astype(jnp.bfloat16)
        rim_mixed[...] = jnp.dot(high, rim, preferred_element_type=jnp.float32) + jnp.dot(
            low, rim, preferred_element_type=jnp.float32
        )

        def rim_part(s, carry):
            for k in sorted({k for _, k, _ in listed}):
                straight = turned = None
                for slot, (j, kk, _source) in enumerate(listed):
                    if kk == k:
                        at = pl.multiple_of((s * len(listed) + slot) * C, C)
                        mixed = rim_mixed[pl.ds(at, C), :]
                        a, b = re_ref[j] * mixed, im_ref[j] * mixed
                        straight = a if straight is None else straight + a
                        turned = b if turned is None else turned + b
                acc_ref[s, k * C : k * C + C] -= swapped(sign * turned) + straight
            return carry

        lax.fori_loop(0, S, rim_part, 0)

    gram_ref[...] = jnp.zeros_like(gram_ref)
    half = 0.5 * mean_in[...].reshape(1, N)
    for part in range(CHUNKS):
        rows = slice(part * CROWS, (part + 1) * CROWS)
        for way, there in ((0, has_l), (1, has_r)):

            @pl.when(there)
            def _():
                plane_copy(way, part).wait_recv()

        sums = [gram_ref[p] for p in range(len(PAIRS))]
        for at in range(0, N, LANES):
            lanes = slice(at, at + LANES)
            gain_l = VISCOSITY + half[:, lanes]
            gain_r = VISCOSITY - half[:, lanes]
            rounded = []
            for s in range(S):
                left = from_left[s, rows, lanes].astype(jnp.float32)
                right = from_right[s, rows, lanes].astype(jnp.float32)
                value = acc_ref[s, rows, lanes] - (gain_l * left + gain_r * right)
                value = value.astype(jnp.bfloat16)
                resp_ref[s, rows, lanes] = value
                rounded.append(value.astype(jnp.float32))
            for p, (s, t) in enumerate(PAIRS):
                product = rounded[s] * rounded[t]
                sums[p] = sums[p] + (product[:C] + product[C:])
        for p in range(len(PAIRS)):
            gram_ref[p] = sums[p]

    row = lax.broadcasted_iota(jnp.int32, (2 * C, 128), 0)
    col = lax.broadcasted_iota(jnp.int32, (2 * C, 128), 1)
    stacked = jnp.zeros((2 * C, 128), jnp.float32)
    hit = row < 0
    for p, (s, t) in enumerate(PAIRS):
        folded = gram_ref[p][:, :128] + gram_ref[p][:, 128:]
        total = jnp.sum(folded, axis=0, keepdims=True)
        stacked = jnp.where(row == p, total, stacked)
        hit = hit | ((row == p) & ((col == S * s + t) | (col == S * t + s)))
    sums = jnp.sum(stacked, axis=1, keepdims=True)
    tile = jnp.sum(jnp.where(hit, sums, 0.0), axis=0, keepdims=True)
    part_ref[...] = tile

    for part in range(CHUNKS):
        for way, there in ((0, has_r), (1, has_l)):

            @pl.when(there)
            def _():
                plane_copy(way, part).wait_send()

    for way, there, far in ((0, has_u, up_hop), (1, has_d, down_hop)):
        split_up = jnp.logical_and(edge, far)

        @when(there, jnp.logical_not(split_up))
        def _():
            rim_copy(way).wait_send()

        @when(split_up)
        def _():
            rim_copy(way, 0, DIRECT).wait_send()
            to_relay(way).wait_send()

        @when(middle, far)
        def _():
            from_relay(way).wait_send()


def apply_operator(forcing, base_harm, mean_flow, mixing, harm_lo, couple_flags):
    hbm, vmem = pl.BlockSpec(memory_space=pltpu.HBM), pl.BlockSpec(memory_space=pltpu.VMEM)
    bf16, f32 = jnp.bfloat16, jnp.float32
    return pl.pallas_call(
        halo_kernel,
        out_shape=(
            pltpu.VMEM((S, ROWS, N), bf16),
            pltpu.VMEM((1, 128), f32),
        ),
        in_specs=[hbm] * 7,
        out_specs=(vmem, vmem),
        scratch_shapes=[
            pltpu.SMEM((4, 4, 7), f32),
            pltpu.SMEM((1,), jnp.int32),
            pltpu.SMEM((K, 7), jnp.int32),
            pltpu.VMEM((S, ROWS, N), bf16),
            pltpu.VMEM((S, ROWS, N), bf16),
            pltpu.VMEM((S, ROWS, N), bf16),
            pltpu.VMEM((2, S, 3, C, N), bf16),
            pltpu.VMEM((S - DIRECT, 3, C, N), bf16),
            pltpu.VMEM((7, 2, 1, N), f32),
            pltpu.VMEM((N,), f32),
            pltpu.VMEM((7, C, N), f32),
            pltpu.VMEM((7, C, N), f32),
            pltpu.VMEM((S, ROWS, N), f32),
            pltpu.VMEM((len(OWN) * C, ROWS), f32),
            pltpu.VMEM((2, S * len(LEFT) * C, S * RIM), f32),
            pltpu.VMEM((len(OWN) * C, N), f32),
            pltpu.VMEM((S * len(LEFT) * C, N), f32),
            pltpu.VMEM((len(PAIRS), C, LANES), f32),
            pltpu.SemaphoreType.DMA((6,)),
            pltpu.SemaphoreType.DMA((2, CHUNKS)),
            pltpu.SemaphoreType.DMA((2, CHUNKS)),
            pltpu.SemaphoreType.DMA((2,)),
            pltpu.SemaphoreType.DMA((2,)),
            pltpu.SemaphoreType.DMA((4,)),
        ],
        compiler_params=pltpu.CompilerParams(
            collective_id=0, has_side_effects=True, vmem_limit_bytes=62 << 20
        ),
        name="operator",
    )(forcing.reshape(S, ROWS, N), forcing.reshape(S, K, C, N), base_harm, mean_flow, mixing, harm_lo, couple_flags)


def solution(mesh):
    n_space, n_freq = mesh.shape["space"], mesh.shape["freq"]
    cells_all = S * K * n_freq * C * n_space * N // S
    y, xh, core, xl = 4, 2, 2, 2
    z = n_space // (xh * y)
    sizes = {"z": z, "xh": xh, "y": y, "xl": xl, "core": core}
    stages = [("xh", "xl", "core"), ("z", "y")]
    counts, orders = [], []

    def hops(axes, step):
        total = 0
        for axis in reversed(axes):
            by = step % sizes[axis]
            total += (2 if axis == "xh" else 1) * min(by, sizes[axis] - by)
            step //= sizes[axis]
        return total

    for axes in stages:
        count = 1
        for axis in axes:
            count *= sizes[axis]
        counts.append(count - 1)
        orders.append(sorted(range(1, count), key=lambda step: -hops(axes, step)))

    def gram_kernel(part_ref, gram_ref, mine, *rest):
        landing, send_sem, recv_sem = rest[:2], rest[2:4], rest[4:6]
        sp, fr = lax.axis_index("space"), lax.axis_index("freq")
        here = {
            "z": sp // (xh * y), "xh": sp // y % xh, "y": sp % y,
            "xl": fr // core, "core": fr % core,
        }

        def partner(axes, step):
            there = dict(here)
            for axis in reversed(axes):
                there[axis] = lax.rem(here[axis] + step % sizes[axis], sizes[axis])
                step //= sizes[axis]
            space = (there["z"] * xh + there["xh"]) * y + there["y"]
            return {"space": space, "freq": there["xl"] * core + there["core"]}

        barrier = pltpu.get_barrier_semaphore()
        for axes, order in zip(stages, orders):
            for step in order:
                pl.semaphore_signal(
                    barrier, inc=1, device_id=partner(axes, step), device_id_type=MESH
                )
        pl.semaphore_wait(barrier, sum(counts))
        total = part_ref[...]
        sent = []
        for i, (axes, order) in enumerate(zip(stages, orders)):
            mine[i] = total
            copies = []
            for step in order:
                copy = pltpu.make_async_remote_copy(
                    src_ref=mine.at[i],
                    dst_ref=landing[i].at[step - 1],
                    send_sem=send_sem[i].at[step - 1],
                    recv_sem=recv_sem[i].at[step - 1],
                    device_id=partner(axes, step),
                    device_id_type=MESH,
                )
                copy.start()
                copies.append(copy)
            for copy in copies:
                copy.wait_recv()
            total = total + jnp.sum(landing[i][...], axis=0)
            sent += copies
        gram_ref[...] = total
        for copy in sent:
            copy.wait_send()

    def finish_kernel(resp_ref, total_ref, out_ref, gram_ref, gram_here, sem):
        copies = [
            pltpu.make_async_copy(resp_ref.at[s], out_ref.at[s], sem.at[s]) for s in range(S)
        ]
        for copy in copies:
            copy.start()
        total = total_ref[...] / cells_all
        row, _col = pair_iota(128)
        tile = jnp.broadcast_to(total, (C, 128))
        for s in range(1, S):
            tile = jnp.where(row == s, pltpu.roll(total, 128 - S * s, 1), tile)
        gram_here[...] = tile[:S, :S]
        copies.append(pltpu.make_async_copy(gram_here, gram_ref, sem.at[S]))
        copies[S].start()
        for copy in copies:
            copy.wait()

    def finish(response, total):
        return pl.pallas_call(
            finish_kernel,
            out_shape=(
                jax.ShapeDtypeStruct(response.shape, response.dtype),
                jax.ShapeDtypeStruct((S, S), jnp.float32),
            ),
            in_specs=[
                pl.BlockSpec(memory_space=pl.ANY),
                pl.BlockSpec(memory_space=pltpu.VMEM),
            ],
            out_specs=(
                pl.BlockSpec(memory_space=pltpu.HBM),
                pl.BlockSpec(memory_space=pltpu.HBM),
            ),
            scratch_shapes=[
                pltpu.VMEM((S, S), jnp.float32),
                pltpu.SemaphoreType.DMA((S + 1,)),
            ],
            compiler_params=pltpu.CompilerParams(vmem_limit_bytes=4 << 20),
            name="finish",
        )(response, total)

    def gram_sum(part):
        f32 = jnp.float32
        return pl.pallas_call(
            gram_kernel,
            out_shape=pltpu.VMEM((1, 128), f32),
            in_specs=[pl.BlockSpec(memory_space=pltpu.VMEM)],
            out_specs=pl.BlockSpec(memory_space=pltpu.VMEM),
            scratch_shapes=[pltpu.VMEM((2, 1, 128), f32)]
            + [pltpu.VMEM((count, 1, 128), f32) for count in counts]
            + [pltpu.SemaphoreType.DMA((count,)) for count in counts] * 2,
            compiler_params=pltpu.CompilerParams(
                collective_id=1, has_side_effects=True, vmem_limit_bytes=4 << 20
            ),
            name="gram_sum",
        )(part)

    def local(forcing, base_harm, mixing, mean_flow, harm_lo, couple_flags):
        shape = forcing.shape
        response, part = apply_operator(
            forcing,
            base_harm,
            mean_flow,
            mixing.transpose(1, 2, 0),
            harm_lo,
            couple_flags,
        )
        response, gram_matrix = finish(response, gram_sum(part))
        return response.reshape(shape), gram_matrix

    return jax.shard_map(
        local,
        mesh=mesh,
        in_specs=(
            P(None, "freq", None, "space", None),
            P(None, None, "space", None),
            P(),
            P(),
            P(),
            P("freq", None),
        ),
        out_specs=(P(None, "freq", None, "space", None), P()),
        check_vma=False,
    )
```

```python
import functools

import jax
import jax.numpy as jnp
from jax import lax
from jax.experimental import pallas as pl
from jax.experimental.pallas import tpu as pltpu
from jax.sharding import PartitionSpec as P

MESH = pl.DeviceIdType.MESH
S, K, C, N = 4, 8, 8, 1536
ROWS = K * C
NZ = 48
OMEGA = 0.05
VISCOSITY = 0.25
CHUNKS = 4
CROWS = ROWS // CHUNKS
RIM = 3 * C
Y = 4
DIRECT = 1
LANES = 256

OWN = [(j, k, k - j + 3) for k in range(K) for j in range(7) if 0 <= k - j + 3 < K]
LEFT = [(j, k, k - j + 6) for k in range(3) for j in range(7) if k - j + 3 < 0]
RIGHT = [(j, k, k - j + 3 - K) for k in range(K - 3, K) for j in range(7) if k - j + 3 >= K]

PAIRS = [(s, t) for s in range(S) for t in range(s, S)]


def split(coeff):
    high = coeff.astype(jnp.bfloat16)
    low = (coeff - high.astype(jnp.float32)).astype(jnp.bfloat16)
    return high, low


def swapped(value):
    return jnp.concatenate([value[4:], value[:4]], axis=0)


def pair_iota(width):
    row = lax.broadcasted_iota(jnp.int32, (C, width), 0)
    col = lax.broadcasted_iota(jnp.int32, (C, width), 1)
    return row, col


def mixing_tile(mix_ref, j, width):
    row, col = pair_iota(width)
    same = (row // 4) == ((col // 4) % 2)
    tile = jnp.zeros((C, width), jnp.float32)
    for v in range(4):
        for w in range(4):
            hit = same & (row % 4 == v) & (col % 4 == w)
            tile = jnp.where(hit, mix_ref[v, w, j], tile)
    return tile


def halo_kernel(
    f_ref, blocks_ref, base_ref, mean_ref, mix_hbm, lo_hbm, flag_hbm, resp_ref, part_ref,
    mix_ref, lo_ref, flag_ref,
    x_ref, from_left, from_right, rim_in, relay, base_in, mean_in, re_ref, im_ref,
    acc_ref, own_coeff, rim_coeff, mixed_ref, rim_mixed, gram_ref,
    in_sem, send_sem, recv_sem, rim_send, rim_recv, relay_sem,
):
    sp, fr = lax.axis_index("space"), lax.axis_index("freq")
    has_l, has_r = sp > 0, sp < lax.axis_size("space") - 1
    has_d, has_u = fr > 0, fr < lax.axis_size("freq") - 1
    to_l, to_r = {"space": sp - 1}, {"space": sp + 1}
    to_d, to_u = {"freq": fr - 1}, {"freq": fr + 1}
    edge = jnp.logical_or(sp % Y == 0, sp % Y == Y - 1)
    middle = jnp.logical_not(edge)
    up_hop, down_hop = fr == 1, fr == 2
    hop = jnp.logical_or(up_hop, down_hop)
    next_row = {"space": sp + 1 - 2 * (sp % 2)}
    across = {"space": sp + 1 - 2 * (sp % 2), "freq": 3 - fr}
    greeted = ((has_l, to_l), (has_r, to_r), (has_d, to_d), (has_u, to_u), (hop, across))

    barrier = pltpu.get_barrier_semaphore()
    for there, device in greeted:

        @pl.when(there)
        def _():
            pl.semaphore_signal(barrier, inc=1, device_id=device, device_id_type=MESH)

    load_x = pltpu.make_async_copy(f_ref, x_ref, in_sem.at[0])
    load_base = pltpu.make_async_copy(base_ref, base_in, in_sem.at[1])
    load_mean = pltpu.make_async_copy(mean_ref, mean_in, in_sem.at[2])
    loads = [load_x, load_base, load_mean]
    for i, (source, target) in enumerate(
        ((mix_hbm, mix_ref), (lo_hbm, lo_ref), (flag_hbm, flag_ref))
    ):
        loads.append(pltpu.make_async_copy(source, target, in_sem.at[3 + i]))
    for load in loads:
        load.start()
    peers = sum(there.astype(jnp.int32) for there, _ in greeted)
    pl.semaphore_wait(barrier, peers)

    def plane_copy(way, part):
        rows = pl.ds(part * CROWS, CROWS)
        landing = from_left if way == 0 else from_right
        return pltpu.make_async_remote_copy(
            src_ref=f_ref.at[:, rows],
            dst_ref=landing.at[:, rows],
            send_sem=send_sem.at[way, part],
            recv_sem=recv_sem.at[way, part],
            device_id=to_r if way == 0 else to_l,
            device_id_type=MESH,
        )

    def rim_of(way, low, high):
        first = K - 3 if way == 0 else 0
        return blocks_ref.at[low:high, first : first + 3]

    def rim_copy(way, low=0, high=S):
        return pltpu.make_async_remote_copy(
            src_ref=rim_of(way, low, high),
            dst_ref=rim_in.at[way, low:high],
            send_sem=rim_send.at[way],
            recv_sem=rim_recv.at[way],
            device_id=to_u if way == 0 else to_d,
            device_id_type=MESH,
        )

    def to_relay(way):
        return pltpu.make_async_remote_copy(
            src_ref=rim_of(way, DIRECT, S),
            dst_ref=relay,
            send_sem=relay_sem.at[0],
            recv_sem=relay_sem.at[1],
            device_id=next_row,
            device_id_type=MESH,
        )

    def from_relay(way):
        return pltpu.make_async_remote_copy(
            src_ref=relay,
            dst_ref=rim_in.at[way, DIRECT:],
            send_sem=relay_sem.at[2],
            recv_sem=relay_sem.at[3],
            device_id=across,
            device_id_type=MESH,
        )

    def when(*conditions):
        return pl.when(functools.reduce(jnp.logical_and, conditions))

    for way, there, far in ((0, has_u, up_hop), (1, has_d, down_hop)):
        split_up = jnp.logical_and(edge, far)

        @when(there, jnp.logical_not(split_up))
        def _():
            rim_copy(way).start()

        @when(split_up)
        def _():
            to_relay(way).start()
            rim_copy(way, 0, DIRECT).start()

    def start_planes(parts):
        for part in parts:
            for way, there in ((0, has_r), (1, has_l)):

                @when(there)
                def _():
                    plane_copy(way, part).start()

    start_planes(range(CHUNKS // 2))

    @when(middle, hop)
    def _():
        to_relay(0).wait_recv()

    for way, far in ((0, up_hop), (1, down_hop)):

        @when(middle, far)
        def _():
            from_relay(way).start()

    start_planes(range(CHUNKS // 2, CHUNKS))

    for way, there in ((0, has_d), (1, has_u)):

        @pl.when(jnp.logical_not(there))
        def _():
            rim_in[way] = jnp.zeros((S, 3, C, N), jnp.bfloat16)

    for landing, there in ((from_left, has_l), (from_right, has_r)):

        @pl.when(jnp.logical_not(there))
        def _():
            landing[...] = jnp.zeros((S, ROWS, N), jnp.bfloat16)

    for load in loads:
        load.wait()
    width = S * RIM
    row, col = pair_iota(width)
    for j in range(7):
        tile = mixing_tile(mix_ref, j, width)
        for slot, (jj, k, source) in enumerate(OWN):
            if jj == j:
                flag = flag_ref[k, j].astype(jnp.float32)
                block = jnp.where(col // C == source, tile, 0.0) * flag
                own_coeff[slot * C : slot * C + C, :] = block[:, :ROWS]
        for way, listed in ((0, LEFT), (1, RIGHT)):
            for slot, (jj, k, source) in enumerate(listed):
                if jj == j:
                    flag = flag_ref[k, j].astype(jnp.float32)
                    for s in range(S):
                        at = (s * len(listed) + slot) * C
                        block = jnp.where(col // C == 3 * s + source, tile, 0.0) * flag
                        rim_coeff[way, at : at + C, :] = block

    for j in range(7):
        re_ref[j] = jnp.broadcast_to(base_in[j, 0], (C, N))
        im_ref[j] = jnp.broadcast_to(base_in[j, 1], (C, N))

    own_high, own_low = split(own_coeff[...])
    own_both = jnp.concatenate([own_high, own_low], axis=1)
    sign = jnp.where(lax.broadcasted_iota(jnp.int32, (C, N), 0) < 4, 1.0, -1.0).astype(jnp.float32)
    first = lo_ref[0] + fr * K

    place = lax.broadcasted_iota(jnp.int32, (C, N), 1)
    span = place % NZ
    span_last, span_first = span == NZ - 1, span == 0
    wake_last, wake_first = place >= N - NZ, place < NZ

    def local_part(s, carry):
        values = x_ref[s]
        mixed_ref[...] = jnp.dot(
            own_both,
            jnp.concatenate([values, values], axis=0),
            preferred_element_type=jnp.float32,
        )
        for k in range(K):
            if k % 2 == 0:
                both = x_ref[s, k * C : k * C + 2 * C].astype(jnp.float32)
            x = both[(k % 2) * C : (k % 2) * C + C]
            up, down = pltpu.roll(x, N - 1, 1), pltpu.roll(x, 1, 1)
            span_up = jnp.where(span_last, pltpu.roll(x, NZ - 1, 1), up)
            span_down = jnp.where(span_first, pltpu.roll(x, N - NZ + 1, 1), down)
            wake_up = jnp.where(wake_last, 0.0, pltpu.roll(x, N - NZ, 1))
            wake_down = jnp.where(wake_first, 0.0, pltpu.roll(x, NZ, 1))
            around = VISCOSITY * (wake_up + wake_down + span_up + span_down - 6.0 * x)
            spin = OMEGA * (first + k).astype(jnp.float32)
            turned = spin * x
            straight = around
            for slot, (j, kk, _source) in enumerate(OWN):
                if kk == k:
                    mixed = mixed_ref[slot * C : slot * C + C, :]
                    straight = straight + re_ref[j] * mixed
                    turned = turned - im_ref[j] * mixed
            acc_ref[s, k * C : k * C + C] = swapped(sign * turned) - straight
        return carry

    lax.fori_loop(0, S, local_part, 0)

    def add_rim(way, there, far, listed):
        split_up = jnp.logical_and(edge, far)

        @when(there, jnp.logical_not(split_up))
        def _():
            rim_copy(way).wait_recv()

        @when(split_up)
        def _():
            rim_copy(way, 0, DIRECT).wait_recv()
            from_relay(way).wait_recv()

        high, low = split(rim_coeff[way])
        rim = rim_in[way].astype(jnp.float32).reshape(S * RIM, N).astype(jnp.bfloat16)
        rim_mixed[...] = jnp.dot(high, rim, preferred_element_type=jnp.float32) + jnp.dot(
            low, rim, preferred_element_type=jnp.float32
        )

        def rim_part(s, carry):
            for k in sorted({k for _, k, _ in listed}):
                straight = turned = None
                for slot, (j, kk, _source) in enumerate(listed):
                    if kk == k:
                        at = pl.multiple_of((s * len(listed) + slot) * C, C)
                        mixed = rim_mixed[pl.ds(at, C), :]
                        a, b = re_ref[j] * mixed, im_ref[j] * mixed
                        straight = a if straight is None else straight + a
                        turned = b if turned is None else turned + b
                acc_ref[s, k * C : k * C + C] -= swapped(sign * turned) + straight
            return carry

        lax.fori_loop(0, S, rim_part, 0)

    gram_ref[...] = jnp.zeros_like(gram_ref)
    half = 0.5 * mean_in[...].reshape(1, N)

    def finish_part(part):
        rows = slice(part * CROWS, (part + 1) * CROWS)
        for way, there in ((0, has_l), (1, has_r)):

            @pl.when(there)
            def _():
                plane_copy(way, part).wait_recv()

        sums = [gram_ref[p] for p in range(len(PAIRS))]
        for at in range(0, N, LANES):
            lanes = slice(at, at + LANES)
            gain_l = VISCOSITY + half[:, lanes]
            gain_r = VISCOSITY - half[:, lanes]
            rounded = []
            for s in range(S):
                left = from_left[s, rows, lanes].astype(jnp.float32)
                right = from_right[s, rows, lanes].astype(jnp.float32)
                value = acc_ref[s, rows, lanes] - (gain_l * left + gain_r * right)
                value = value.astype(jnp.bfloat16)
                resp_ref[s, rows, lanes] = value
                rounded.append(value.astype(jnp.float32))
            for p, (s, t) in enumerate(PAIRS):
                product = rounded[s] * rounded[t]
                sums[p] = sums[p] + (product[:C] + product[C:])
        for p in range(len(PAIRS)):
            gram_ref[p] = sums[p]

    for way, there, far, listed in ((0, has_d, down_hop, LEFT), (1, has_u, up_hop, RIGHT)):
        add_rim(way, there, far, listed)
        for part in range(way * (CHUNKS // 2), (way + 1) * (CHUNKS // 2)):
            finish_part(part)

    row = lax.broadcasted_iota(jnp.int32, (2 * C, 128), 0)
    col = lax.broadcasted_iota(jnp.int32, (2 * C, 128), 1)
    stacked = jnp.zeros((2 * C, 128), jnp.float32)
    hit = row < 0
    for p, (s, t) in enumerate(PAIRS):
        folded = gram_ref[p][:, :128] + gram_ref[p][:, 128:]
        total = jnp.sum(folded, axis=0, keepdims=True)
        stacked = jnp.where(row == p, total, stacked)
        hit = hit | ((row == p) & ((col == S * s + t) | (col == S * t + s)))
    sums = jnp.sum(stacked, axis=1, keepdims=True)
    tile = jnp.sum(jnp.where(hit, sums, 0.0), axis=0, keepdims=True)
    part_ref[...] = tile

    for part in range(CHUNKS):
        for way, there in ((0, has_r), (1, has_l)):

            @pl.when(there)
            def _():
                plane_copy(way, part).wait_send()

    for way, there, far in ((0, has_u, up_hop), (1, has_d, down_hop)):
        split_up = jnp.logical_and(edge, far)

        @when(there, jnp.logical_not(split_up))
        def _():
            rim_copy(way).wait_send()

        @when(split_up)
        def _():
            rim_copy(way, 0, DIRECT).wait_send()
            to_relay(way).wait_send()

        @when(middle, far)
        def _():
            from_relay(way).wait_send()


def apply_operator(forcing, base_harm, mean_flow, mixing, harm_lo, couple_flags):
    hbm, vmem = pl.BlockSpec(memory_space=pltpu.HBM), pl.BlockSpec(memory_space=pltpu.VMEM)
    bf16, f32 = jnp.bfloat16, jnp.float32
    return pl.pallas_call(
        halo_kernel,
        out_shape=(
            pltpu.VMEM((S, ROWS, N), bf16),
            pltpu.VMEM((1, 128), f32),
        ),
        in_specs=[hbm] * 7,
        out_specs=(vmem, vmem),
        scratch_shapes=[
            pltpu.SMEM((4, 4, 7), f32),
            pltpu.SMEM((1,), jnp.int32),
            pltpu.SMEM((K, 7), jnp.int32),
            pltpu.VMEM((S, ROWS, N), bf16),
            pltpu.VMEM((S, ROWS, N), bf16),
            pltpu.VMEM((S, ROWS, N), bf16),
            pltpu.VMEM((2, S, 3, C, N), bf16),
            pltpu.VMEM((S - DIRECT, 3, C, N), bf16),
            pltpu.VMEM((7, 2, 1, N), f32),
            pltpu.VMEM((N,), f32),
            pltpu.VMEM((7, C, N), f32),
            pltpu.VMEM((7, C, N), f32),
            pltpu.VMEM((S, ROWS, N), f32),
            pltpu.VMEM((len(OWN) * C, ROWS), f32),
            pltpu.VMEM((2, S * len(LEFT) * C, S * RIM), f32),
            pltpu.VMEM((len(OWN) * C, N), f32),
            pltpu.VMEM((S * len(LEFT) * C, N), f32),
            pltpu.VMEM((len(PAIRS), C, LANES), f32),
            pltpu.SemaphoreType.DMA((6,)),
            pltpu.SemaphoreType.DMA((2, CHUNKS)),
            pltpu.SemaphoreType.DMA((2, CHUNKS)),
            pltpu.SemaphoreType.DMA((2,)),
            pltpu.SemaphoreType.DMA((2,)),
            pltpu.SemaphoreType.DMA((4,)),
        ],
        compiler_params=pltpu.CompilerParams(
            collective_id=0, has_side_effects=True, vmem_limit_bytes=62 << 20
        ),
        name="operator",
    )(forcing.reshape(S, ROWS, N), forcing.reshape(S, K, C, N), base_harm, mean_flow, mixing, harm_lo, couple_flags)


def solution(mesh):
    n_space, n_freq = mesh.shape["space"], mesh.shape["freq"]
    cells_all = S * K * n_freq * C * n_space * N // S
    y, xh, core, xl = 4, 2, 2, 2
    z = n_space // (xh * y)
    sizes = {"z": z, "xh": xh, "y": y, "xl": xl, "core": core}
    stages = [("xh", "xl", "core"), ("z", "y")]
    counts, orders = [], []

    def hops(axes, step):
        total = 0
        for axis in reversed(axes):
            by = step % sizes[axis]
            total += (2 if axis == "xh" else 1) * min(by, sizes[axis] - by)
            step //= sizes[axis]
        return total

    for axes in stages:
        count = 1
        for axis in axes:
            count *= sizes[axis]
        counts.append(count - 1)
        orders.append(sorted(range(1, count), key=lambda step: -hops(axes, step)))

    def gram_kernel(part_ref, gram_ref, mine, *rest):
        landing, send_sem, recv_sem = rest[:2], rest[2:4], rest[4:6]
        sp, fr = lax.axis_index("space"), lax.axis_index("freq")
        here = {
            "z": sp // (xh * y), "xh": sp // y % xh, "y": sp % y,
            "xl": fr // core, "core": fr % core,
        }

        def partner(axes, step):
            there = dict(here)
            for axis in reversed(axes):
                there[axis] = lax.rem(here[axis] + step % sizes[axis], sizes[axis])
                step //= sizes[axis]
            space = (there["z"] * xh + there["xh"]) * y + there["y"]
            return {"space": space, "freq": there["xl"] * core + there["core"]}

        barrier = pltpu.get_barrier_semaphore()
        for axes, order in zip(stages, orders):
            for step in order:
                pl.semaphore_signal(
                    barrier, inc=1, device_id=partner(axes, step), device_id_type=MESH
                )
        pl.semaphore_wait(barrier, sum(counts))
        total = part_ref[...]
        sent = []
        for i, (axes, order) in enumerate(zip(stages, orders)):
            mine[i] = total
            copies = []
            for step in order:
                copy = pltpu.make_async_remote_copy(
                    src_ref=mine.at[i],
                    dst_ref=landing[i].at[step - 1],
                    send_sem=send_sem[i].at[step - 1],
                    recv_sem=recv_sem[i].at[step - 1],
                    device_id=partner(axes, step),
                    device_id_type=MESH,
                )
                copy.start()
                copies.append(copy)
            for copy in copies:
                copy.wait_recv()
            total = total + jnp.sum(landing[i][...], axis=0)
            sent += copies
        gram_ref[...] = total
        for copy in sent:
            copy.wait_send()

    def finish_kernel(resp_ref, total_ref, out_ref, gram_ref, gram_here, sem):
        copies = [
            pltpu.make_async_copy(resp_ref.at[s], out_ref.at[s], sem.at[s]) for s in range(S)
        ]
        for copy in copies:
            copy.start()
        total = total_ref[...] / cells_all
        row, _col = pair_iota(128)
        tile = jnp.broadcast_to(total, (C, 128))
        for s in range(1, S):
            tile = jnp.where(row == s, pltpu.roll(total, 128 - S * s, 1), tile)
        gram_here[...] = tile[:S, :S]
        copies.append(pltpu.make_async_copy(gram_here, gram_ref, sem.at[S]))
        copies[S].start()
        for copy in copies:
            copy.wait()

    def finish(response, total):
        return pl.pallas_call(
            finish_kernel,
            out_shape=(
                jax.ShapeDtypeStruct(response.shape, response.dtype),
                jax.ShapeDtypeStruct((S, S), jnp.float32),
            ),
            in_specs=[
                pl.BlockSpec(memory_space=pl.ANY),
                pl.BlockSpec(memory_space=pltpu.VMEM),
            ],
            out_specs=(
                pl.BlockSpec(memory_space=pltpu.HBM),
                pl.BlockSpec(memory_space=pltpu.HBM),
            ),
            scratch_shapes=[
                pltpu.VMEM((S, S), jnp.float32),
                pltpu.SemaphoreType.DMA((S + 1,)),
            ],
            compiler_params=pltpu.CompilerParams(vmem_limit_bytes=4 << 20),
            name="finish",
        )(response, total)

    def gram_sum(part):
        f32 = jnp.float32
        return pl.pallas_call(
            gram_kernel,
            out_shape=pltpu.VMEM((1, 128), f32),
            in_specs=[pl.BlockSpec(memory_space=pltpu.VMEM)],
            out_specs=pl.BlockSpec(memory_space=pltpu.VMEM),
            scratch_shapes=[pltpu.VMEM((2, 1, 128), f32)]
            + [pltpu.VMEM((count, 1, 128), f32) for count in counts]
            + [pltpu.SemaphoreType.DMA((count,)) for count in counts] * 2,
            compiler_params=pltpu.CompilerParams(
                collective_id=1, has_side_effects=True, vmem_limit_bytes=4 << 20
            ),
            name="gram_sum",
        )(part)

    def local(forcing, base_harm, mixing, mean_flow, harm_lo, couple_flags):
        shape = forcing.shape
        response, part = apply_operator(
            forcing,
            base_harm,
            mean_flow,
            mixing.transpose(1, 2, 0),
            harm_lo,
            couple_flags,
        )
        response, gram_matrix = finish(response, gram_sum(part))
        return response.reshape(shape), gram_matrix

    return jax.shard_map(
        local,
        mesh=mesh,
        in_specs=(
            P(None, "freq", None, "space", None),
            P(None, None, "space", None),
            P(),
            P(),
            P(),
            P("freq", None),
        ),
        out_specs=(P(None, "freq", None, "space", None), P()),
        check_vma=False,
    )
```

```python
import functools

import jax
import jax.numpy as jnp
from jax import lax
from jax.experimental import pallas as pl
from jax.experimental.pallas import tpu as pltpu
from jax.sharding import PartitionSpec as P

MESH = pl.DeviceIdType.MESH
S, K, C, N = 4, 8, 8, 1536
ROWS = K * C
NZ = 48
OMEGA = 0.05
VISCOSITY = 0.25
CHUNKS = 4
CROWS = ROWS // CHUNKS
RIM = 3 * C
Y = 4
DIRECT = 1
LANES = 256

OWN = [(j, k, k - j + 3) for k in range(K) for j in range(7) if 0 <= k - j + 3 < K]
LEFT = [(j, k, k - j + 6) for k in range(3) for j in range(7) if k - j + 3 < 0]
RIGHT = [(j, k, k - j + 3 - K) for k in range(K - 3, K) for j in range(7) if k - j + 3 >= K]

PAIRS = [(s, t) for s in range(S) for t in range(s, S)]


def split(coeff):
    high = coeff.astype(jnp.bfloat16)
    low = (coeff - high.astype(jnp.float32)).astype(jnp.bfloat16)
    return high, low


def swapped(value):
    return jnp.concatenate([value[4:], value[:4]], axis=0)


def pair_iota(width):
    row = lax.broadcasted_iota(jnp.int32, (C, width), 0)
    col = lax.broadcasted_iota(jnp.int32, (C, width), 1)
    return row, col


def mixing_tile(mix_ref, j, width):
    row, col = pair_iota(width)
    same = (row // 4) == ((col // 4) % 2)
    tile = jnp.zeros((C, width), jnp.float32)
    for v in range(4):
        for w in range(4):
            hit = same & (row % 4 == v) & (col % 4 == w)
            tile = jnp.where(hit, mix_ref[v, w, j], tile)
    return tile


def halo_kernel(
    f_ref, blocks_ref, base_ref, mean_ref, mix_hbm, lo_hbm, flag_hbm, resp_ref, part_ref,
    mix_ref, lo_ref, flag_ref,
    x_ref, from_left, from_right, rim_in, relay, base_in, mean_in, re_ref, im_ref,
    acc_ref, own_coeff, rim_coeff, mixed_ref, rim_mixed, gram_ref,
    in_sem, send_sem, recv_sem, rim_send, rim_recv, relay_sem,
):
    sp, fr = lax.axis_index("space"), lax.axis_index("freq")
    has_l, has_r = sp > 0, sp < lax.axis_size("space") - 1
    has_d, has_u = fr > 0, fr < lax.axis_size("freq") - 1
    to_l, to_r = {"space": sp - 1}, {"space": sp + 1}
    to_d, to_u = {"freq": fr - 1}, {"freq": fr + 1}
    edge = jnp.logical_or(sp % Y == 0, sp % Y == Y - 1)
    middle = jnp.logical_not(edge)
    up_hop, down_hop = fr == 1, fr == 2
    hop = jnp.logical_or(up_hop, down_hop)
    next_row = {"space": sp + 1 - 2 * (sp % 2)}
    across = {"space": sp + 1 - 2 * (sp % 2), "freq": 3 - fr}
    greeted = ((has_l, to_l), (has_r, to_r), (has_d, to_d), (has_u, to_u), (hop, across))

    barrier = pltpu.get_barrier_semaphore()
    for there, device in greeted:

        @pl.when(there)
        def _():
            pl.semaphore_signal(barrier, inc=1, device_id=device, device_id_type=MESH)

    load_x = pltpu.make_async_copy(f_ref, x_ref, in_sem.at[0])
    load_base = pltpu.make_async_copy(base_ref, base_in, in_sem.at[1])
    load_mean = pltpu.make_async_copy(mean_ref, mean_in, in_sem.at[2])
    loads = [load_x, load_base, load_mean]
    for i, (source, target) in enumerate(
        ((mix_hbm, mix_ref), (lo_hbm, lo_ref), (flag_hbm, flag_ref))
    ):
        loads.append(pltpu.make_async_copy(source, target, in_sem.at[3 + i]))
    for load in loads:
        load.start()
    peers = sum(there.astype(jnp.int32) for there, _ in greeted)
    pl.semaphore_wait(barrier, peers)

    def plane_copy(way, part):
        rows = pl.ds(part * CROWS, CROWS)
        landing = from_left if way == 0 else from_right
        return pltpu.make_async_remote_copy(
            src_ref=f_ref.at[:, rows],
            dst_ref=landing.at[:, rows],
            send_sem=send_sem.at[way, part],
            recv_sem=recv_sem.at[way, part],
            device_id=to_r if way == 0 else to_l,
            device_id_type=MESH,
        )

    def rim_of(way, low, high):
        first = K - 3 if way == 0 else 0
        return blocks_ref.at[low:high, first : first + 3]

    def rim_copy(way, low=0, high=S):
        return pltpu.make_async_remote_copy(
            src_ref=rim_of(way, low, high),
            dst_ref=rim_in.at[way, low:high],
            send_sem=rim_send.at[way],
            recv_sem=rim_recv.at[way],
            device_id=to_u if way == 0 else to_d,
            device_id_type=MESH,
        )

    def to_relay(way):
        return pltpu.make_async_remote_copy(
            src_ref=rim_of(way, DIRECT, S),
            dst_ref=relay,
            send_sem=relay_sem.at[0],
            recv_sem=relay_sem.at[1],
            device_id=next_row,
            device_id_type=MESH,
        )

    def from_relay(way):
        return pltpu.make_async_remote_copy(
            src_ref=relay,
            dst_ref=rim_in.at[way, DIRECT:],
            send_sem=relay_sem.at[2],
            recv_sem=relay_sem.at[3],
            device_id=across,
            device_id_type=MESH,
        )

    def when(*conditions):
        return pl.when(functools.reduce(jnp.logical_and, conditions))

    for way, there, far in ((0, has_u, up_hop), (1, has_d, down_hop)):
        split_up = jnp.logical_and(edge, far)

        @when(there, jnp.logical_not(split_up))
        def _():
            rim_copy(way).start()

        @when(split_up)
        def _():
            to_relay(way).start()
            rim_copy(way, 0, DIRECT).start()

    def start_planes(parts):
        for part in parts:
            for way, there in ((0, has_r), (1, has_l)):

                @when(there)
                def _():
                    plane_copy(way, part).start()

    start_planes(range(CHUNKS // 2))

    @when(middle, hop)
    def _():
        to_relay(0).wait_recv()

    for way, far in ((0, up_hop), (1, down_hop)):

        @when(middle, far)
        def _():
            from_relay(way).start()

    start_planes(range(CHUNKS // 2, CHUNKS))

    for way, there in ((0, has_d), (1, has_u)):

        @pl.when(jnp.logical_not(there))
        def _():
            rim_in[way] = jnp.zeros((S, 3, C, N), jnp.bfloat16)

    for landing, there in ((from_left, has_l), (from_right, has_r)):

        @pl.when(jnp.logical_not(there))
        def _():
            landing[...] = jnp.zeros((S, ROWS, N), jnp.bfloat16)

    for load in loads:
        load.wait()
    width = S * RIM
    row, col = pair_iota(width)
    for j in range(7):
        tile = mixing_tile(mix_ref, j, width)
        for slot, (jj, k, source) in enumerate(OWN):
            if jj == j:
                flag = flag_ref[k, j].astype(jnp.float32)
                block = jnp.where(col // C == source, tile, 0.0) * flag
                own_coeff[slot * C : slot * C + C, :] = block[:, :ROWS]
        for way, listed in ((0, LEFT), (1, RIGHT)):
            for slot, (jj, k, source) in enumerate(listed):
                if jj == j:
                    flag = flag_ref[k, j].astype(jnp.float32)
                    for s in range(S):
                        at = (s * len(listed) + slot) * C
                        block = jnp.where(col // C == 3 * s + source, tile, 0.0) * flag
                        rim_coeff[way, at : at + C, :] = block

    for j in range(7):
        re_ref[j] = jnp.broadcast_to(base_in[j, 0], (C, N))
        im_ref[j] = jnp.broadcast_to(base_in[j, 1], (C, N))

    own_high, own_low = split(own_coeff[...])
    own_both = jnp.concatenate([own_high, own_low], axis=1)
    sign = jnp.where(lax.broadcasted_iota(jnp.int32, (C, N), 0) < 4, 1.0, -1.0).astype(jnp.float32)
    first = lo_ref[0] + fr * K

    place = lax.broadcasted_iota(jnp.int32, (C, N), 1)
    span = place % NZ
    span_last, span_first = span == NZ - 1, span == 0
    wake_last, wake_first = place >= N - NZ, place < NZ

    def local_part(s, carry):
        values = x_ref[s]
        mixed_ref[...] = jnp.dot(
            own_both,
            jnp.concatenate([values, values], axis=0),
            preferred_element_type=jnp.float32,
        )
        for k in range(K):
            if k % 2 == 0:
                both = x_ref[s, k * C : k * C + 2 * C].astype(jnp.float32)
            x = both[(k % 2) * C : (k % 2) * C + C]
            up, down = pltpu.roll(x, N - 1, 1), pltpu.roll(x, 1, 1)
            span_up = jnp.where(span_last, pltpu.roll(x, NZ - 1, 1), up)
            span_down = jnp.where(span_first, pltpu.roll(x, N - NZ + 1, 1), down)
            wake_up = jnp.where(wake_last, 0.0, pltpu.roll(x, N - NZ, 1))
            wake_down = jnp.where(wake_first, 0.0, pltpu.roll(x, NZ, 1))
            around = VISCOSITY * (wake_up + wake_down + span_up + span_down - 6.0 * x)
            spin = OMEGA * (first + k).astype(jnp.float32)
            turned = spin * x
            straight = around
            for slot, (j, kk, _source) in enumerate(OWN):
                if kk == k:
                    mixed = mixed_ref[slot * C : slot * C + C, :]
                    straight = straight + re_ref[j] * mixed
                    turned = turned - im_ref[j] * mixed
            acc_ref[s, k * C : k * C + C] = swapped(sign * turned) - straight
        return carry

    lax.fori_loop(0, S, local_part, 0)

    def add_rim(way, there, far, listed):
        split_up = jnp.logical_and(edge, far)

        @when(there, jnp.logical_not(split_up))
        def _():
            rim_copy(way).wait_recv()

        @when(split_up)
        def _():
            rim_copy(way, 0, DIRECT).wait_recv()
            from_relay(way).wait_recv()

        high, low = split(rim_coeff[way])
        rim = rim_in[way].astype(jnp.float32).reshape(S * RIM, N).astype(jnp.bfloat16)
        rim_mixed[...] = jnp.dot(high, rim, preferred_element_type=jnp.float32) + jnp.dot(
            low, rim, preferred_element_type=jnp.float32
        )

        def rim_part(s, carry):
            for k in sorted({k for _, k, _ in listed}):
                straight = turned = None
                for slot, (j, kk, _source) in enumerate(listed):
                    if kk == k:
                        at = pl.multiple_of((s * len(listed) + slot) * C, C)
                        mixed = rim_mixed[pl.ds(at, C), :]
                        a, b = re_ref[j] * mixed, im_ref[j] * mixed
                        straight = a if straight is None else straight + a
                        turned = b if turned is None else turned + b
                acc_ref[s, k * C : k * C + C] -= swapped(sign * turned) + straight
            return carry

        lax.fori_loop(0, S, rim_part, 0)

    gram_ref[...] = jnp.zeros_like(gram_ref)
    half = 0.5 * mean_in[...].reshape(1, N)

    def finish_part(part):
        rows = slice(part * CROWS, (part + 1) * CROWS)
        for way, there in ((0, has_l), (1, has_r)):

            @pl.when(there)
            def _():
                plane_copy(way, part).wait_recv()

        sums = [gram_ref[p] for p in range(len(PAIRS))]
        for at in range(0, N, LANES):
            lanes = slice(at, at + LANES)
            gain_l = VISCOSITY + half[:, lanes]
            gain_r = VISCOSITY - half[:, lanes]
            rounded = []
            for s in range(S):
                left = from_left[s, rows, lanes].astype(jnp.float32)
                right = from_right[s, rows, lanes].astype(jnp.float32)
                value = acc_ref[s, rows, lanes] - (gain_l * left + gain_r * right)
                value = value.astype(jnp.bfloat16)
                resp_ref[s, rows, lanes] = value
                rounded.append(value.astype(jnp.float32))
            for p, (s, t) in enumerate(PAIRS):
                product = rounded[s] * rounded[t]
                sums[p] = sums[p] + (product[:C] + product[C:])
        for p in range(len(PAIRS)):
            gram_ref[p] = sums[p]

    for way, there, far, listed in ((0, has_d, down_hop, LEFT), (1, has_u, up_hop, RIGHT)):
        add_rim(way, there, far, listed)
        for part in range(way * (CHUNKS // 2), (way + 1) * (CHUNKS // 2)):
            finish_part(part)

    row = lax.broadcasted_iota(jnp.int32, (2 * C, 128), 0)
    col = lax.broadcasted_iota(jnp.int32, (2 * C, 128), 1)
    stacked = jnp.zeros((2 * C, 128), jnp.float32)
    hit = row < 0
    for p, (s, t) in enumerate(PAIRS):
        folded = gram_ref[p][:, :128] + gram_ref[p][:, 128:]
        total = jnp.sum(folded, axis=0, keepdims=True)
        stacked = jnp.where(row == p, total, stacked)
        hit = hit | ((row == p) & ((col == S * s + t) | (col == S * t + s)))
    sums = jnp.sum(stacked, axis=1, keepdims=True)
    tile = jnp.sum(jnp.where(hit, sums, 0.0), axis=0, keepdims=True)
    part_ref[...] = tile

    for part in range(CHUNKS):
        for way, there in ((0, has_r), (1, has_l)):

            @pl.when(there)
            def _():
                plane_copy(way, part).wait_send()

    for way, there, far in ((0, has_u, up_hop), (1, has_d, down_hop)):
        split_up = jnp.logical_and(edge, far)

        @when(there, jnp.logical_not(split_up))
        def _():
            rim_copy(way).wait_send()

        @when(split_up)
        def _():
            rim_copy(way, 0, DIRECT).wait_send()
            to_relay(way).wait_send()

        @when(middle, far)
        def _():
            from_relay(way).wait_send()


def apply_operator(forcing, base_harm, mean_flow, mixing, harm_lo, couple_flags):
    hbm, vmem = pl.BlockSpec(memory_space=pltpu.HBM), pl.BlockSpec(memory_space=pltpu.VMEM)
    bf16, f32 = jnp.bfloat16, jnp.float32
    return pl.pallas_call(
        halo_kernel,
        out_shape=(
            pltpu.VMEM((S, ROWS, N), bf16),
            pltpu.VMEM((1, 128), f32),
        ),
        in_specs=[hbm] * 7,
        out_specs=(vmem, vmem),
        scratch_shapes=[
            pltpu.SMEM((4, 4, 7), f32),
            pltpu.SMEM((1,), jnp.int32),
            pltpu.SMEM((K, 7), jnp.int32),
            pltpu.VMEM((S, ROWS, N), bf16),
            pltpu.VMEM((S, ROWS, N), bf16),
            pltpu.VMEM((S, ROWS, N), bf16),
            pltpu.VMEM((2, S, 3, C, N), bf16),
            pltpu.VMEM((S - DIRECT, 3, C, N), bf16),
            pltpu.VMEM((7, 2, 1, N), f32),
            pltpu.VMEM((N,), f32),
            pltpu.VMEM((7, C, N), f32),
            pltpu.VMEM((7, C, N), f32),
            pltpu.VMEM((S, ROWS, N), f32),
            pltpu.VMEM((len(OWN) * C, ROWS), f32),
            pltpu.VMEM((2, S * len(LEFT) * C, S * RIM), f32),
            pltpu.VMEM((len(OWN) * C, N), f32),
            pltpu.VMEM((S * len(LEFT) * C, N), f32),
            pltpu.VMEM((len(PAIRS), C, LANES), f32),
            pltpu.SemaphoreType.DMA((6,)),
            pltpu.SemaphoreType.DMA((2, CHUNKS)),
            pltpu.SemaphoreType.DMA((2, CHUNKS)),
            pltpu.SemaphoreType.DMA((2,)),
            pltpu.SemaphoreType.DMA((2,)),
            pltpu.SemaphoreType.DMA((4,)),
        ],
        compiler_params=pltpu.CompilerParams(
            collective_id=0, has_side_effects=True, vmem_limit_bytes=62 << 20
        ),
        name="operator",
    )(forcing.reshape(S, ROWS, N), forcing.reshape(S, K, C, N), base_harm, mean_flow, mixing, harm_lo, couple_flags)


def solution(mesh):
    n_space, n_freq = mesh.shape["space"], mesh.shape["freq"]
    cells_all = S * K * n_freq * C * n_space * N // S
    y, xh, core, xl = 4, 2, 2, 2
    z = n_space // (xh * y)
    sizes = {"z": z, "xh": xh, "y": y, "xl": xl, "core": core}
    stages = [("z", "y"), ("xh", "xl", "core")]
    counts, orders = [], []

    def hops(axes, step):
        total = 0
        for axis in reversed(axes):
            by = step % sizes[axis]
            total += (2 if axis == "xh" else 1) * min(by, sizes[axis] - by)
            step //= sizes[axis]
        return total

    for axes in stages:
        count = 1
        for axis in axes:
            count *= sizes[axis]
        counts.append(count - 1)
        orders.append(sorted(range(1, count), key=lambda step: -hops(axes, step)))

    def gram_kernel(part_ref, gram_ref, mine, *rest):
        landing, send_sem, recv_sem = rest[:2], rest[2:4], rest[4:6]
        sp, fr = lax.axis_index("space"), lax.axis_index("freq")
        here = {
            "z": sp // (xh * y), "xh": sp // y % xh, "y": sp % y,
            "xl": fr // core, "core": fr % core,
        }

        def partner(axes, step):
            there = dict(here)
            for axis in reversed(axes):
                there[axis] = lax.rem(here[axis] + step % sizes[axis], sizes[axis])
                step //= sizes[axis]
            space = (there["z"] * xh + there["xh"]) * y + there["y"]
            return {"space": space, "freq": there["xl"] * core + there["core"]}

        barrier = pltpu.get_barrier_semaphore()
        for axes, order in zip(stages, orders):
            for step in order:
                pl.semaphore_signal(
                    barrier, inc=1, device_id=partner(axes, step), device_id_type=MESH
                )
        pl.semaphore_wait(barrier, sum(counts))
        total = part_ref[...]
        sent = []
        for i, (axes, order) in enumerate(zip(stages, orders)):
            mine[i] = total
            copies = []
            for step in order:
                copy = pltpu.make_async_remote_copy(
                    src_ref=mine.at[i],
                    dst_ref=landing[i].at[step - 1],
                    send_sem=send_sem[i].at[step - 1],
                    recv_sem=recv_sem[i].at[step - 1],
                    device_id=partner(axes, step),
                    device_id_type=MESH,
                )
                copy.start()
                copies.append(copy)
            for copy in copies:
                copy.wait_recv()
            total = total + jnp.sum(landing[i][...], axis=0)
            sent += copies
        gram_ref[...] = total
        for copy in sent:
            copy.wait_send()

    def finish_kernel(resp_ref, total_ref, out_ref, gram_ref, gram_here, sem):
        copies = [
            pltpu.make_async_copy(resp_ref.at[s], out_ref.at[s], sem.at[s]) for s in range(S)
        ]
        for copy in copies:
            copy.start()
        total = total_ref[...] / cells_all
        row, _col = pair_iota(128)
        tile = jnp.broadcast_to(total, (C, 128))
        for s in range(1, S):
            tile = jnp.where(row == s, pltpu.roll(total, 128 - S * s, 1), tile)
        gram_here[...] = tile[:S, :S]
        copies.append(pltpu.make_async_copy(gram_here, gram_ref, sem.at[S]))
        copies[S].start()
        for copy in copies:
            copy.wait()

    def finish(response, total):
        return pl.pallas_call(
            finish_kernel,
            out_shape=(
                jax.ShapeDtypeStruct(response.shape, response.dtype),
                jax.ShapeDtypeStruct((S, S), jnp.float32),
            ),
            in_specs=[
                pl.BlockSpec(memory_space=pl.ANY),
                pl.BlockSpec(memory_space=pltpu.VMEM),
            ],
            out_specs=(
                pl.BlockSpec(memory_space=pltpu.HBM),
                pl.BlockSpec(memory_space=pltpu.HBM),
            ),
            scratch_shapes=[
                pltpu.VMEM((S, S), jnp.float32),
                pltpu.SemaphoreType.DMA((S + 1,)),
            ],
            compiler_params=pltpu.CompilerParams(vmem_limit_bytes=4 << 20),
            name="finish",
        )(response, total)

    def gram_sum(part):
        f32 = jnp.float32
        return pl.pallas_call(
            gram_kernel,
            out_shape=pltpu.VMEM((1, 128), f32),
            in_specs=[pl.BlockSpec(memory_space=pltpu.VMEM)],
            out_specs=pl.BlockSpec(memory_space=pltpu.VMEM),
            scratch_shapes=[pltpu.VMEM((2, 1, 128), f32)]
            + [pltpu.VMEM((count, 1, 128), f32) for count in counts]
            + [pltpu.SemaphoreType.DMA((count,)) for count in counts] * 2,
            compiler_params=pltpu.CompilerParams(
                collective_id=1, has_side_effects=True, vmem_limit_bytes=4 << 20
            ),
            name="gram_sum",
        )(part)

    def local(forcing, base_harm, mixing, mean_flow, harm_lo, couple_flags):
        shape = forcing.shape
        response, part = apply_operator(
            forcing,
            base_harm,
            mean_flow,
            mixing.transpose(1, 2, 0),
            harm_lo,
            couple_flags,
        )
        response, gram_matrix = finish(response, gram_sum(part))
        return response.reshape(shape), gram_matrix

    return jax.shard_map(
        local,
        mesh=mesh,
        in_specs=(
            P(None, "freq", None, "space", None),
            P(None, None, "space", None),
            P(),
            P(),
            P(),
            P("freq", None),
        ),
        out_specs=(P(None, "freq", None, "space", None), P()),
        check_vma=False,
    )
```

```python
import functools

import jax
import jax.numpy as jnp
from jax import lax
from jax.experimental import pallas as pl
from jax.experimental.pallas import tpu as pltpu
from jax.sharding import PartitionSpec as P

MESH = pl.DeviceIdType.MESH
S, K, C, N = 4, 8, 8, 1536
ROWS = K * C
NZ = 48
OMEGA = 0.05
VISCOSITY = 0.25
CHUNKS = 4
CROWS = ROWS // CHUNKS
RIM = 3 * C
Y = 4
DIRECT = 1
LANES = 256

OWN = [(j, k, k - j + 3) for k in range(K) for j in range(7) if 0 <= k - j + 3 < K]
LEFT = [(j, k, k - j + 6) for k in range(3) for j in range(7) if k - j + 3 < 0]
RIGHT = [(j, k, k - j + 3 - K) for k in range(K - 3, K) for j in range(7) if k - j + 3 >= K]

PAIRS = [(s, t) for s in range(S) for t in range(s, S)]


def split(coeff):
    high = coeff.astype(jnp.bfloat16)
    low = (coeff - high.astype(jnp.float32)).astype(jnp.bfloat16)
    return high, low


def swapped(value):
    return jnp.concatenate([value[4:], value[:4]], axis=0)


def pair_iota(width):
    row = lax.broadcasted_iota(jnp.int32, (C, width), 0)
    col = lax.broadcasted_iota(jnp.int32, (C, width), 1)
    return row, col


def mixing_tile(mix_ref, j, width):
    row, col = pair_iota(width)
    same = (row // 4) == ((col // 4) % 2)
    tile = jnp.zeros((C, width), jnp.float32)
    for v in range(4):
        for w in range(4):
            hit = same & (row % 4 == v) & (col % 4 == w)
            tile = jnp.where(hit, mix_ref[v, w, j], tile)
    return tile


def halo_kernel(
    f_ref, blocks_ref, base_ref, mean_ref, mix_hbm, lo_hbm, flag_hbm, resp_ref, part_ref,
    mix_ref, lo_ref, flag_ref,
    x_ref, from_left, from_right, rim_in, relay, base_in, mean_in, re_ref, im_ref,
    acc_ref, own_coeff, rim_coeff, mixed_ref, rim_mixed, gram_ref,
    in_sem, send_sem, recv_sem, rim_send, rim_recv, relay_sem,
):
    sp, fr = lax.axis_index("space"), lax.axis_index("freq")
    has_l, has_r = sp > 0, sp < lax.axis_size("space") - 1
    has_d, has_u = fr > 0, fr < lax.axis_size("freq") - 1
    to_l, to_r = {"space": sp - 1}, {"space": sp + 1}
    to_d, to_u = {"freq": fr - 1}, {"freq": fr + 1}
    edge = jnp.logical_or(sp % Y == 0, sp % Y == Y - 1)
    middle = jnp.logical_not(edge)
    up_hop, down_hop = fr == 1, fr == 2
    hop = jnp.logical_or(up_hop, down_hop)
    next_row = {"space": sp + 1 - 2 * (sp % 2)}
    across = {"space": sp + 1 - 2 * (sp % 2), "freq": 3 - fr}
    greeted = ((has_l, to_l), (has_r, to_r), (has_d, to_d), (has_u, to_u), (hop, across))

    barrier = pltpu.get_barrier_semaphore()
    for there, device in greeted:

        @pl.when(there)
        def _():
            pl.semaphore_signal(barrier, inc=1, device_id=device, device_id_type=MESH)

    load_x = pltpu.make_async_copy(f_ref, x_ref, in_sem.at[0])
    load_base = pltpu.make_async_copy(base_ref, base_in, in_sem.at[1])
    load_mean = pltpu.make_async_copy(mean_ref, mean_in, in_sem.at[2])
    loads = [load_x, load_base, load_mean]
    for i, (source, target) in enumerate(
        ((mix_hbm, mix_ref), (lo_hbm, lo_ref), (flag_hbm, flag_ref))
    ):
        loads.append(pltpu.make_async_copy(source, target, in_sem.at[3 + i]))
    peers = sum(there.astype(jnp.int32) for there, _ in greeted)
    pl.semaphore_wait(barrier, peers)

    def plane_copy(way, part):
        rows = pl.ds(part * CROWS, CROWS)
        landing = from_left if way == 0 else from_right
        return pltpu.make_async_remote_copy(
            src_ref=f_ref.at[:, rows],
            dst_ref=landing.at[:, rows],
            send_sem=send_sem.at[way, part],
            recv_sem=recv_sem.at[way, part],
            device_id=to_r if way == 0 else to_l,
            device_id_type=MESH,
        )

    def rim_of(way, low, high):
        first = K - 3 if way == 0 else 0
        return blocks_ref.at[low:high, first : first + 3]

    def rim_copy(way, low=0, high=S):
        return pltpu.make_async_remote_copy(
            src_ref=rim_of(way, low, high),
            dst_ref=rim_in.at[way, low:high],
            send_sem=rim_send.at[way],
            recv_sem=rim_recv.at[way],
            device_id=to_u if way == 0 else to_d,
            device_id_type=MESH,
        )

    def to_relay(way):
        return pltpu.make_async_remote_copy(
            src_ref=rim_of(way, DIRECT, S),
            dst_ref=relay,
            send_sem=relay_sem.at[0],
            recv_sem=relay_sem.at[1],
            device_id=next_row,
            device_id_type=MESH,
        )

    def from_relay(way):
        return pltpu.make_async_remote_copy(
            src_ref=relay,
            dst_ref=rim_in.at[way, DIRECT:],
            send_sem=relay_sem.at[2],
            recv_sem=relay_sem.at[3],
            device_id=across,
            device_id_type=MESH,
        )

    def when(*conditions):
        return pl.when(functools.reduce(jnp.logical_and, conditions))

    for way, there, far in ((0, has_u, up_hop), (1, has_d, down_hop)):
        split_up = jnp.logical_and(edge, far)

        @when(there, jnp.logical_not(split_up))
        def _():
            rim_copy(way).start()

        @when(split_up)
        def _():
            to_relay(way).start()
            rim_copy(way, 0, DIRECT).start()

    def start_planes(parts):
        for part in parts:
            for way, there in ((0, has_r), (1, has_l)):

                @when(there)
                def _():
                    plane_copy(way, part).start()

    start_planes(range(CHUNKS // 2))
    for load in loads:
        load.start()

    @when(middle, hop)
    def _():
        to_relay(0).wait_recv()

    for way, far in ((0, up_hop), (1, down_hop)):

        @when(middle, far)
        def _():
            from_relay(way).start()

    start_planes(range(CHUNKS // 2, CHUNKS))

    for way, there in ((0, has_d), (1, has_u)):

        @pl.when(jnp.logical_not(there))
        def _():
            rim_in[way] = jnp.zeros((S, 3, C, N), jnp.bfloat16)

    for landing, there in ((from_left, has_l), (from_right, has_r)):

        @pl.when(jnp.logical_not(there))
        def _():
            landing[...] = jnp.zeros((S, ROWS, N), jnp.bfloat16)

    for load in loads:
        load.wait()
    width = S * RIM
    row, col = pair_iota(width)
    for j in range(7):
        tile = mixing_tile(mix_ref, j, width)
        for slot, (jj, k, source) in enumerate(OWN):
            if jj == j:
                flag = flag_ref[k, j].astype(jnp.float32)
                block = jnp.where(col // C == source, tile, 0.0) * flag
                own_coeff[slot * C : slot * C + C, :] = block[:, :ROWS]
        for way, listed in ((0, LEFT), (1, RIGHT)):
            for slot, (jj, k, source) in enumerate(listed):
                if jj == j:
                    flag = flag_ref[k, j].astype(jnp.float32)
                    for s in range(S):
                        at = (s * len(listed) + slot) * C
                        block = jnp.where(col // C == 3 * s + source, tile, 0.0) * flag
                        rim_coeff[way, at : at + C, :] = block

    for j in range(7):
        re_ref[j] = jnp.broadcast_to(base_in[j, 0], (C, N))
        im_ref[j] = jnp.broadcast_to(base_in[j, 1], (C, N))

    own_high, own_low = split(own_coeff[...])
    own_both = jnp.concatenate([own_high, own_low], axis=1)
    sign = jnp.where(lax.broadcasted_iota(jnp.int32, (C, N), 0) < 4, 1.0, -1.0).astype(jnp.float32)
    first = lo_ref[0] + fr * K

    place = lax.broadcasted_iota(jnp.int32, (C, N), 1)
    span = place % NZ
    span_last, span_first = span == NZ - 1, span == 0
    wake_last, wake_first = place >= N - NZ, place < NZ

    def local_part(s, carry):
        values = x_ref[s]
        mixed_ref[...] = jnp.dot(
            own_both,
            jnp.concatenate([values, values], axis=0),
            preferred_element_type=jnp.float32,
        )
        for k in range(K):
            if k % 2 == 0:
                both = x_ref[s, k * C : k * C + 2 * C].astype(jnp.float32)
            x = both[(k % 2) * C : (k % 2) * C + C]
            up, down = pltpu.roll(x, N - 1, 1), pltpu.roll(x, 1, 1)
            span_up = jnp.where(span_last, pltpu.roll(x, NZ - 1, 1), up)
            span_down = jnp.where(span_first, pltpu.roll(x, N - NZ + 1, 1), down)
            wake_up = jnp.where(wake_last, 0.0, pltpu.roll(x, N - NZ, 1))
            wake_down = jnp.where(wake_first, 0.0, pltpu.roll(x, NZ, 1))
            around = VISCOSITY * (wake_up + wake_down + span_up + span_down - 6.0 * x)
            spin = OMEGA * (first + k).astype(jnp.float32)
            turned = spin * x
            straight = around
            for slot, (j, kk, _source) in enumerate(OWN):
                if kk == k:
                    mixed = mixed_ref[slot * C : slot * C + C, :]
                    straight = straight + re_ref[j] * mixed
                    turned = turned - im_ref[j] * mixed
            acc_ref[s, k * C : k * C + C] = swapped(sign * turned) - straight
        return carry

    lax.fori_loop(0, S, local_part, 0)

    def add_rim(way, there, far, listed):
        split_up = jnp.logical_and(edge, far)

        @when(there, jnp.logical_not(split_up))
        def _():
            rim_copy(way).wait_recv()

        @when(split_up)
        def _():
            rim_copy(way, 0, DIRECT).wait_recv()
            from_relay(way).wait_recv()

        high, low = split(rim_coeff[way])
        rim = rim_in[way].astype(jnp.float32).reshape(S * RIM, N).astype(jnp.bfloat16)
        rim_mixed[...] = jnp.dot(high, rim, preferred_element_type=jnp.float32) + jnp.dot(
            low, rim, preferred_element_type=jnp.float32
        )

        def rim_part(s, carry):
            for k in sorted({k for _, k, _ in listed}):
                straight = turned = None
                for slot, (j, kk, _source) in enumerate(listed):
                    if kk == k:
                        at = pl.multiple_of((s * len(listed) + slot) * C, C)
                        mixed = rim_mixed[pl.ds(at, C), :]
                        a, b = re_ref[j] * mixed, im_ref[j] * mixed
                        straight = a if straight is None else straight + a
                        turned = b if turned is None else turned + b
                acc_ref[s, k * C : k * C + C] -= swapped(sign * turned) + straight
            return carry

        lax.fori_loop(0, S, rim_part, 0)

    gram_ref[...] = jnp.zeros_like(gram_ref)
    half = 0.5 * mean_in[...].reshape(1, N)

    def finish_part(part):
        rows = slice(part * CROWS, (part + 1) * CROWS)
        for way, there in ((0, has_l), (1, has_r)):

            @pl.when(there)
            def _():
                plane_copy(way, part).wait_recv()

        sums = [gram_ref[p] for p in range(len(PAIRS))]
        for at in range(0, N, LANES):
            lanes = slice(at, at + LANES)
            gain_l = VISCOSITY + half[:, lanes]
            gain_r = VISCOSITY - half[:, lanes]
            rounded = []
            for s in range(S):
                left = from_left[s, rows, lanes].astype(jnp.float32)
                right = from_right[s, rows, lanes].astype(jnp.float32)
                value = acc_ref[s, rows, lanes] - (gain_l * left + gain_r * right)
                value = value.astype(jnp.bfloat16)
                resp_ref[s, rows, lanes] = value
                rounded.append(value.astype(jnp.float32))
            for p, (s, t) in enumerate(PAIRS):
                product = rounded[s] * rounded[t]
                sums[p] = sums[p] + (product[:C] + product[C:])
        for p in range(len(PAIRS)):
            gram_ref[p] = sums[p]

    for way, there, far, listed in ((0, has_d, down_hop, LEFT), (1, has_u, up_hop, RIGHT)):
        add_rim(way, there, far, listed)
        for part in range(way * (CHUNKS // 2), (way + 1) * (CHUNKS // 2)):
            finish_part(part)

    row = lax.broadcasted_iota(jnp.int32, (2 * C, 128), 0)
    col = lax.broadcasted_iota(jnp.int32, (2 * C, 128), 1)
    stacked = jnp.zeros((2 * C, 128), jnp.float32)
    hit = row < 0
    for p, (s, t) in enumerate(PAIRS):
        folded = gram_ref[p][:, :128] + gram_ref[p][:, 128:]
        total = jnp.sum(folded, axis=0, keepdims=True)
        stacked = jnp.where(row == p, total, stacked)
        hit = hit | ((row == p) & ((col == S * s + t) | (col == S * t + s)))
    sums = jnp.sum(stacked, axis=1, keepdims=True)
    tile = jnp.sum(jnp.where(hit, sums, 0.0), axis=0, keepdims=True)
    part_ref[...] = tile

    for part in range(CHUNKS):
        for way, there in ((0, has_r), (1, has_l)):

            @pl.when(there)
            def _():
                plane_copy(way, part).wait_send()

    for way, there, far in ((0, has_u, up_hop), (1, has_d, down_hop)):
        split_up = jnp.logical_and(edge, far)

        @when(there, jnp.logical_not(split_up))
        def _():
            rim_copy(way).wait_send()

        @when(split_up)
        def _():
            rim_copy(way, 0, DIRECT).wait_send()
            to_relay(way).wait_send()

        @when(middle, far)
        def _():
            from_relay(way).wait_send()


def apply_operator(forcing, base_harm, mean_flow, mixing, harm_lo, couple_flags):
    hbm, vmem = pl.BlockSpec(memory_space=pltpu.HBM), pl.BlockSpec(memory_space=pltpu.VMEM)
    bf16, f32 = jnp.bfloat16, jnp.float32
    return pl.pallas_call(
        halo_kernel,
        out_shape=(
            pltpu.VMEM((S, ROWS, N), bf16),
            pltpu.VMEM((1, 128), f32),
        ),
        in_specs=[hbm] * 7,
        out_specs=(vmem, vmem),
        scratch_shapes=[
            pltpu.SMEM((4, 4, 7), f32),
            pltpu.SMEM((1,), jnp.int32),
            pltpu.SMEM((K, 7), jnp.int32),
            pltpu.VMEM((S, ROWS, N), bf16),
            pltpu.VMEM((S, ROWS, N), bf16),
            pltpu.VMEM((S, ROWS, N), bf16),
            pltpu.VMEM((2, S, 3, C, N), bf16),
            pltpu.VMEM((S - DIRECT, 3, C, N), bf16),
            pltpu.VMEM((7, 2, 1, N), f32),
            pltpu.VMEM((N,), f32),
            pltpu.VMEM((7, C, N), f32),
            pltpu.VMEM((7, C, N), f32),
            pltpu.VMEM((S, ROWS, N), f32),
            pltpu.VMEM((len(OWN) * C, ROWS), f32),
            pltpu.VMEM((2, S * len(LEFT) * C, S * RIM), f32),
            pltpu.VMEM((len(OWN) * C, N), f32),
            pltpu.VMEM((S * len(LEFT) * C, N), f32),
            pltpu.VMEM((len(PAIRS), C, LANES), f32),
            pltpu.SemaphoreType.DMA((6,)),
            pltpu.SemaphoreType.DMA((2, CHUNKS)),
            pltpu.SemaphoreType.DMA((2, CHUNKS)),
            pltpu.SemaphoreType.DMA((2,)),
            pltpu.SemaphoreType.DMA((2,)),
            pltpu.SemaphoreType.DMA((4,)),
        ],
        compiler_params=pltpu.CompilerParams(
            collective_id=0, has_side_effects=True, vmem_limit_bytes=62 << 20
        ),
        name="operator",
    )(forcing.reshape(S, ROWS, N), forcing.reshape(S, K, C, N), base_harm, mean_flow, mixing, harm_lo, couple_flags)


def solution(mesh):
    n_space, n_freq = mesh.shape["space"], mesh.shape["freq"]
    cells_all = S * K * n_freq * C * n_space * N // S
    y, xh, core, xl = 4, 2, 2, 2
    z = n_space // (xh * y)
    sizes = {"z": z, "xh": xh, "y": y, "xl": xl, "core": core}
    stages = [("xh", "xl", "core"), ("z", "y")]
    counts, orders = [], []

    def hops(axes, step):
        total = 0
        for axis in reversed(axes):
            by = step % sizes[axis]
            total += (2 if axis == "xh" else 1) * min(by, sizes[axis] - by)
            step //= sizes[axis]
        return total

    for axes in stages:
        count = 1
        for axis in axes:
            count *= sizes[axis]
        counts.append(count - 1)
        orders.append(sorted(range(1, count), key=lambda step: -hops(axes, step)))

    def gram_kernel(part_ref, gram_ref, mine, *rest):
        landing, send_sem, recv_sem = rest[:2], rest[2:4], rest[4:6]
        sp, fr = lax.axis_index("space"), lax.axis_index("freq")
        here = {
            "z": sp // (xh * y), "xh": sp // y % xh, "y": sp % y,
            "xl": fr // core, "core": fr % core,
        }

        def partner(axes, step):
            there = dict(here)
            for axis in reversed(axes):
                there[axis] = lax.rem(here[axis] + step % sizes[axis], sizes[axis])
                step //= sizes[axis]
            space = (there["z"] * xh + there["xh"]) * y + there["y"]
            return {"space": space, "freq": there["xl"] * core + there["core"]}

        barrier = pltpu.get_barrier_semaphore()
        for axes, order in zip(stages, orders):
            for step in order:
                pl.semaphore_signal(
                    barrier, inc=1, device_id=partner(axes, step), device_id_type=MESH
                )
        pl.semaphore_wait(barrier, sum(counts))
        total = part_ref[...]
        sent = []
        for i, (axes, order) in enumerate(zip(stages, orders)):
            mine[i] = total
            copies = []
            for step in order:
                copy = pltpu.make_async_remote_copy(
                    src_ref=mine.at[i],
                    dst_ref=landing[i].at[step - 1],
                    send_sem=send_sem[i].at[step - 1],
                    recv_sem=recv_sem[i].at[step - 1],
                    device_id=partner(axes, step),
                    device_id_type=MESH,
                )
                copy.start()
                copies.append(copy)
            for copy in copies:
                copy.wait_recv()
            total = total + jnp.sum(landing[i][...], axis=0)
            sent += copies
        gram_ref[...] = total
        for copy in sent:
            copy.wait_send()

    def finish_kernel(resp_ref, total_ref, out_ref, gram_ref, gram_here, sem):
        copies = [
            pltpu.make_async_copy(resp_ref.at[s], out_ref.at[s], sem.at[s]) for s in range(S)
        ]
        for copy in copies:
            copy.start()
        total = total_ref[...] / cells_all
        row, _col = pair_iota(128)
        tile = jnp.broadcast_to(total, (C, 128))
        for s in range(1, S):
            tile = jnp.where(row == s, pltpu.roll(total, 128 - S * s, 1), tile)
        gram_here[...] = tile[:S, :S]
        copies.append(pltpu.make_async_copy(gram_here, gram_ref, sem.at[S]))
        copies[S].start()
        for copy in copies:
            copy.wait()

    def finish(response, total):
        return pl.pallas_call(
            finish_kernel,
            out_shape=(
                jax.ShapeDtypeStruct(response.shape, response.dtype),
                jax.ShapeDtypeStruct((S, S), jnp.float32),
            ),
            in_specs=[
                pl.BlockSpec(memory_space=pl.ANY),
                pl.BlockSpec(memory_space=pltpu.VMEM),
            ],
            out_specs=(
                pl.BlockSpec(memory_space=pltpu.HBM),
                pl.BlockSpec(memory_space=pltpu.HBM),
            ),
            scratch_shapes=[
                pltpu.VMEM((S, S), jnp.float32),
                pltpu.SemaphoreType.DMA((S + 1,)),
            ],
            compiler_params=pltpu.CompilerParams(vmem_limit_bytes=4 << 20),
            name="finish",
        )(response, total)

    def gram_sum(part):
        f32 = jnp.float32
        return pl.pallas_call(
            gram_kernel,
            out_shape=pltpu.VMEM((1, 128), f32),
            in_specs=[pl.BlockSpec(memory_space=pltpu.VMEM)],
            out_specs=pl.BlockSpec(memory_space=pltpu.VMEM),
            scratch_shapes=[pltpu.VMEM((2, 1, 128), f32)]
            + [pltpu.VMEM((count, 1, 128), f32) for count in counts]
            + [pltpu.SemaphoreType.DMA((count,)) for count in counts] * 2,
            compiler_params=pltpu.CompilerParams(
                collective_id=1, has_side_effects=True, vmem_limit_bytes=4 << 20
            ),
            name="gram_sum",
        )(part)

    def local(forcing, base_harm, mixing, mean_flow, harm_lo, couple_flags):
        shape = forcing.shape
        response, part = apply_operator(
            forcing,
            base_harm,
            mean_flow,
            mixing.transpose(1, 2, 0),
            harm_lo,
            couple_flags,
        )
        response, gram_matrix = finish(response, gram_sum(part))
        return response.reshape(shape), gram_matrix

    return jax.shard_map(
        local,
        mesh=mesh,
        in_specs=(
            P(None, "freq", None, "space", None),
            P(None, None, "space", None),
            P(),
            P(),
            P(),
            P("freq", None),
        ),
        out_specs=(P(None, "freq", None, "space", None), P()),
        check_vma=False,
    )
```
